32 devices in a mesh: groups: 2 (over y), tile: 16 (over z, x, core).
Axes of the slice: x: 2, y: 2, z: 4, core: 2. Of those that a mesh axis runs over, the one named last changes fastest.
Arguments:
- level_map: int32 [16], replicated, may hold values from 0 to 7, as said below
- loc_lat: bfloat16 [256, 256], replicated, may hold values from -0.1875 to 0.1875
- loc_lon: bfloat16 [256, 256], replicated, may hold values from -0.1875 to 0.1875
- ens_perts: bfloat16 [32, 256, 256], P(('groups', 'tile')), parts along dimension 0, may hold values from -4 to 4
- ens_control: float32 [32, 256, 256], P(('groups', 'tile')), parts along dimension 0, may hold values from -6 to 6
- static_control: float32 [16, 256, 256], P('groups', 'tile'), parts along dimension 0, may hold values from -6 to 6
- static_scale: float32 [16, 256, 256], P('groups', 'tile'), parts along dimension 0, may hold values from 0.3 to 1.5
- coefs: float32 [4, 16, 256, 256], P(None, 'groups', 'tile'), parts along dimension 1, may hold values from 0.02 to 0.24
- obs_weight: float32 [3, 16, 256, 256], P(None, 'groups', 'tile'), parts along dimension 1, may hold values from 0.05 to 0.5
- innovation: float32 [3, 16, 256, 256], P(None, 'groups', 'tile'), parts along dimension 1, may hold values from -6 to 6
Outputs:
- ens_final: float32 [32, 256, 256], P(('groups', 'tile')), parts along dimension 0
- static_final: float32 [16, 256, 256], P('groups', 'tile'), parts along dimension 0
The draws below stay inside these ranges and needn't reach their ends.
There are 2 independent parts, one for each index of `groups`. The reference program is written for one: setup_inputs(seed, part) draws one part's arguments, and reference() takes and returns one part's arrays. A program takes and returns all parts, laid end to end along the dimension named above; an argument that names none is the same for every part. Nothing has to cross between parts.
Inputs may be any that keep to these rules, and one draw needn't show every extreme that they name: `level_map`: each of the 8 levels is named by exactly 2 entries.
All inputs are finite; a program needn't handle non-finite values.
Results may differ from the reference program's by a relative error of at most 0.0003.
Values sent between devices are 32-bit elements; how exact they have to be, the bound alone decides.
A program may use at most 64 MiB of HBM per device.

```python
import math
import jax
import jax.numpy as jnp
from jax import lax

NLAT = 256
NLON = 256
LEV = 8
MEM_DEV = 1
STEPS = 3
ITERS = 1
GROUP_DEV = 2
MEMBERS = 2
BLOCKS = 16
N_TILE = 16


def draw_level_map(key, part):
    levels_sorted = jnp.repeat(jnp.arange(LEV, dtype=jnp.int32), GROUP_DEV)
    return jax.random.permutation(jax.random.fold_in(key, 7), levels_sorted)


def block_levels(key, dims, split, least, largest):
    level, own = 1.0, jax.random.fold_in(key, 6)
    for position, parts in split:
        draws = jnp.exp(jax.random.uniform(jax.random.fold_in(own, position), (parts,), jnp.float32, least / len(split), largest / len(split)))
        level = level * jnp.repeat(draws, dims[position] // parts).reshape([-1 if axis == position else 1 for axis in range(len(dims))])
    return level


def centred(rng, shape, width, reach, split=(), held_as=jnp.bfloat16):
    result = jax.random.normal(rng, shape, jnp.float32) * width
    if len(split) > 0:
        result = block_levels(rng, shape, split, -0.22, 0.18) * result
    return jnp.clip(result, min=-reach, max=reach).astype(held_as)


def setup_inputs(seed: int = 0, part: int = 0) -> dict:
    arg_keys = jax.random.split(jax.random.key(seed), 11)
    part_splits = jax.random.split(jax.random.fold_in(arg_keys[10], part), 11)
    return {
        "level_map": draw_level_map(jax.random.fold_in(arg_keys[10], 71), part),
        "loc_lat": centred(arg_keys[1], (NLAT, NLAT), (4 * NLAT) ** -0.5, 0.1875),
        "loc_lon": centred(arg_keys[2], (NLON, NLON), (4 * NLON) ** -0.5, 0.1875),
        "ens_perts": centred(part_splits[3], (BLOCKS, NLAT, NLON), (MEMBERS ** -0.5), 4.0, ((0, 16),)),
        "ens_control": centred(part_splits[4], (BLOCKS, NLAT, NLON), 1.0, 6.0, ((0, 16),), jnp.float32),
        "static_control": centred(part_splits[5], (LEV, NLAT, NLON), 1.0, 6.0, ((1, 16),), jnp.float32),
        "static_scale": jnp.clip(jnp.exp(math.log(1.5) - 1.60943787 * jax.random.uniform(part_splits[6], (LEV, NLAT, NLON), jnp.float32) ** block_levels(part_splits[6], (LEV, NLAT, NLON), ((1, 16),), -0.2, 0.2)), 0.3, 1.5),
        "coefs": jnp.clip(0.02 + 0.22 * jax.random.uniform(part_splits[7], (4, LEV, NLAT, NLON), jnp.float32) ** block_levels(part_splits[7], (4, LEV, NLAT, NLON), ((2, 16),), -0.2, 0.2), 0.02, 0.24),
        "obs_weight": jnp.clip(jnp.exp(math.log(0.5) - 2.3025851 * jax.random.uniform(part_splits[8], (STEPS, LEV, NLAT, NLON), jnp.float32) ** block_levels(part_splits[8], (STEPS, LEV, NLAT, NLON), ((2, 16),), -0.2, 0.2)), 0.05, 0.5),
        "innovation": centred(part_splits[9], (STEPS, LEV, NLAT, NLON), 1.0, 6.0, ((2, 16),), jnp.float32),
    }


step_size = 0.15


def rounded(values):
    return lax.optimization_barrier(values.astype(jnp.bfloat16)).astype(jnp.float32)


def forward_step(state, coeffs):
    padded = jnp.pad(state, ((0, 0), (1, 1), (0, 0)))
    north_rows = padded[:, 2:]
    south_rows = padded[:, :-2]
    east_cells = jnp.roll(state, -1, 2)
    west_cells = jnp.roll(state, 1, 2)
    return state + coeffs[0] * (north_rows - state) + coeffs[1] * (south_rows - state) + coeffs[2] * (east_cells - state) + coeffs[3] * (west_cells - state)


def adjoint_step(adjoint, coeffs):
    coef_sum = coeffs[0] + coeffs[1] + coeffs[2] + coeffs[3]
    north_flux = jnp.pad(coeffs[0] * adjoint, ((0, 0), (1, 1), (0, 0)))[:, :-2]
    south_flux = jnp.pad(coeffs[1] * adjoint, ((0, 0), (1, 1), (0, 0)))[:, 2:]
    return (1.0 - coef_sum) * adjoint + north_flux + south_flux + jnp.roll(coeffs[2] * adjoint, 1, 2) + jnp.roll(coeffs[3] * adjoint, -1, 2)


def window_gradient(total_incr, coefs, obs_weight, innovation):
    state = total_incr
    weighted = []
    for section in range(STEPS):
        state = forward_step(state, coefs)
        weighted.append(obs_weight[section] * (state - innovation[section]))
    adjoint = weighted[STEPS - 1]
    for section in range(STEPS - 2, -1, -1):
        adjoint = adjoint_step(adjoint, coefs) + weighted[section]
    return adjoint_step(adjoint, coefs)


def reference(level_map, loc_lat, loc_lon, ens_perts, ens_control, static_control, static_scale, coefs, obs_weight, innovation):
    lat_matrix = loc_lat.astype(jnp.float32)
    lon_matrix = loc_lon.astype(jnp.float32)
    perts = ens_perts.reshape(N_TILE, MEM_DEV, NLAT, NLON)
    level_onehot = (level_map[:, None] == jnp.arange(LEV, dtype=jnp.int32)[None, :]).astype(jnp.float32)

    def member_sum(operands):
        members, control = operands
        lat_smoothed = rounded(jnp.einsum('ij,bjk->bik', lat_matrix, rounded(control)))
        member_field = jnp.einsum('bij,kj->bik', lat_smoothed, lon_matrix)
        return jnp.sum(members.astype(jnp.float32) * member_field, axis=0)

    def member_update(operands):
        members, control, grad_field = operands
        weighted_grad = rounded(members.astype(jnp.float32) * grad_field[None])
        adjoint_lat = rounded(jnp.einsum('ji,bjk->bik', lat_matrix, weighted_grad))
        member_grad = jnp.einsum('bij,jk->bik', adjoint_lat, lon_matrix)
        return control - step_size * (control + member_grad)

    control = ens_control.reshape(N_TILE, MEM_DEV, NLAT, NLON)
    for sweep in range(ITERS):
        partials = lax.map(member_sum, (perts, control))
        ens_incr = jnp.einsum('dl,dij->lij', level_onehot, partials, precision=lax.Precision.HIGHEST)
        total_incr = static_scale * static_control + ens_incr
        gradient = window_gradient(total_incr, coefs, obs_weight, innovation)
        static_control = static_control - step_size * (static_control + static_scale * gradient)
        grad_fields = jnp.take(gradient, level_map, axis=0)
        control = lax.map(member_update, (perts, control, grad_fields))
    return control.reshape(BLOCKS, NLAT, NLON), static_control
```

```python
import functools

import jax
import jax.numpy as jnp
from jax import lax
from jax.experimental import pallas as pl
from jax.experimental.pallas import tpu as pltpu
from jax.sharding import PartitionSpec as P

STEPS = 3


step_size = 0.15


def extended(block, sides, width):
    for axis, dim in sides:
        count = lax.axis_size(axis)
        forward = [(i, i + 1) for i in range(count - 1)]
        backward = [(target, source) for source, target in forward]
        low = lax.ppermute(
            lax.slice_in_dim(block, block.shape[dim] - width, None, axis=dim), axis, forward
        )
        high = lax.ppermute(lax.slice_in_dim(block, 0, width, axis=dim), axis, backward)
        block = jnp.concatenate([low, block, high], axis=dim)
    return block


def forward_step(state, coeffs):
    padded = extended(state, (("tile", 1),), 1)
    north_rows = padded[:, 2:]
    south_rows = padded[:, :-2]
    east_cells = jnp.roll(state, -1, 2)
    west_cells = jnp.roll(state, 1, 2)
    return (
        state
        + coeffs[0] * (north_rows - state)
        + coeffs[1] * (south_rows - state)
        + coeffs[2] * (east_cells - state)
        + coeffs[3] * (west_cells - state)
    )


def adjoint_step(adjoint, coeffs):
    coef_sum = coeffs[0] + coeffs[1] + coeffs[2] + coeffs[3]
    fluxes = jnp.stack([coeffs[0] * adjoint, coeffs[1] * adjoint])
    padded = extended(fluxes, (("tile", 2),), 1)
    north_flux = padded[0][:, :-2]
    south_flux = padded[1][:, 2:]
    return (
        (1.0 - coef_sum) * adjoint
        + north_flux
        + south_flux
        + jnp.roll(coeffs[2] * adjoint, 1, 2)
        + jnp.roll(coeffs[3] * adjoint, -1, 2)
    )


def window_gradient(total_incr, coefs, obs_weight, innovation):
    state = total_incr
    weighted = []
    for section in range(STEPS):
        state = forward_step(state, coefs)
        weighted.append(obs_weight[section] * (state - innovation[section]))
    adjoint = weighted[STEPS - 1]
    for section in range(STEPS - 2, -1, -1):
        adjoint = adjoint_step(adjoint, coefs) + weighted[section]
    return adjoint_step(adjoint, coefs)


def local(
    level_map,
    loc_lat,
    loc_lon,
    ens_perts,
    ens_control,
    static_control,
    static_scale,
    coefs,
    obs_weight,
    innovation,
):
    tile_count = lax.axis_size("tile")
    my_level = level_map[lax.axis_index("tile")]
    levels = static_control.shape[0]
    level_ids = jnp.arange(levels, dtype=jnp.int32)
    level_onehot = (level_map[:, None] == level_ids[None, :]).astype(jnp.float32)
    control = ens_control
    lat_smoothed = jnp.einsum(
        "ij,bjk->bik", loc_lat, control.astype(jnp.bfloat16), preferred_element_type=jnp.float32
    ).astype(jnp.bfloat16)
    member_field = jnp.einsum(
        "bij,kj->bik", lat_smoothed, loc_lon, preferred_element_type=jnp.float32
    )
    partial_value = jnp.sum(ens_perts.astype(jnp.float32) * member_field, axis=0)
    pieces = partial_value.reshape(tile_count, -1, partial_value.shape[1])
    received = lax.all_to_all(pieces, "tile", split_axis=0, concat_axis=0, tiled=True)
    ens_incr = jnp.einsum("dl,dij->lij", level_onehot, received, precision=lax.Precision.HIGHEST)
    total_incr = static_scale * static_control + ens_incr
    gradient = window_gradient(total_incr, coefs, obs_weight, innovation)
    static_control = static_control - step_size * (static_control + static_scale * gradient)
    gathered = lax.all_gather(gradient, "tile", axis=1, tiled=True)
    grad_field = lax.dynamic_index_in_dim(gathered, my_level, 0, keepdims=False)
    weighted_grad = (ens_perts.astype(jnp.float32) * grad_field[None]).astype(jnp.bfloat16)
    adjoint_lat = jnp.einsum(
        "ji,bjk->bik", loc_lat, weighted_grad, preferred_element_type=jnp.float32
    ).astype(jnp.bfloat16)
    member_grad = jnp.einsum(
        "bij,jk->bik", adjoint_lat, loc_lon, preferred_element_type=jnp.float32
    )
    control = control - step_size * (control + member_grad)
    return (control, static_control)


MESH = pl.DeviceIdType.MESH
SIDE = 4


def kernel(
    n,
    level_map,
    lat_hbm,
    lon_hbm,
    perts_hbm,
    control_hbm,
    static_hbm,
    scale_hbm,
    coefs_hbm,
    weight_hbm,
    innov_hbm,
    ens_out,
    static_out,
    lat,
    lon,
    perts,
    control,
    static,
    scale,
    coefs,
    weight,
    innov,
    lat_t,
    field,
    received,
    coef_win,
    keep_win,
    total_win,
    weight_win,
    innov_win,
    weighted,
    early_send,
    early_recv,
    late_send,
    late_recv,
    grad,
    grad_send,
    grad_field,
    ens_new,
    static_new,
    in_sem,
    out_sem,
    member_send_sem,
    member_recv_sem,
    early_send_sem,
    early_recv_sem,
    late_send_sem,
    late_recv_sem,
    grad_send_sem,
    grad_recv_sem,
):
    me = lax.axis_index("tile")
    levels, rows, cols = static.shape
    nlat = control.shape[0]
    win = rows + 2 * SIDE
    main = slice(SIDE, SIDE + rows)

    loads = {}
    for place, (name, source, target) in enumerate(
        (
            ("control", control_hbm.at[0], control),
            ("lat", lat_hbm, lat),
            ("lon", lon_hbm, lon),
            ("perts", perts_hbm.at[0], perts),
            ("coefs", coefs_hbm, coefs),
            ("static", static_hbm, static),
            ("scale", scale_hbm, scale),
            ("weight", weight_hbm, weight),
            ("innov", innov_hbm, innov),
        )
    ):
        loads[name] = pltpu.make_async_copy(source, target, in_sem.at[place])
        loads[name].start()

    barrier = pltpu.get_barrier_semaphore()
    for d in range(1, n):
        pl.semaphore_signal(
            barrier, inc=1, device_id={"tile": lax.rem(me + d, n)}, device_id_type=MESH
        )

    loads["control"].wait()
    loads["lat"].wait()
    smoothed = jnp.dot(
        lat[...], control[...].astype(jnp.bfloat16), preferred_element_type=jnp.float32
    ).astype(jnp.bfloat16)
    loads["lon"].wait()
    member = lax.dot_general(
        smoothed, lon[...], (((1,), (1,)), ((), ())), preferred_element_type=jnp.float32
    )
    loads["perts"].wait()
    field[0:SIDE, :] = jnp.zeros((SIDE, cols), jnp.float32)
    field[SIDE + nlat : 2 * SIDE + nlat, :] = jnp.zeros((SIDE, cols), jnp.float32)
    field[SIDE : SIDE + nlat, :] = perts[...].astype(jnp.float32) * member

    pl.semaphore_wait(barrier, n - 1)

    def window(tile):
        return pl.ds(pl.multiple_of(tile * rows, 8), win)

    member_copies = []
    for d in range(1, n):
        peer = lax.rem(me + d, n)
        copy = pltpu.make_async_remote_copy(
            src_ref=field.at[window(peer)],
            dst_ref=received.at[me],
            send_sem=member_send_sem.at[d],
            recv_sem=member_recv_sem.at[d],
            device_id={"tile": peer},
            device_id_type=MESH,
        )
        copy.start()
        member_copies.append(copy)
    received[me] = field[window(me), :]

    loads["coefs"].wait()
    loads["static"].wait()
    loads["scale"].wait()
    for level in range(levels):
        values = [coefs[k, level] for k in range(4)] + [scale[level] * static[level]]
        for k, value in enumerate(values):
            at = (k * levels + level) * SIDE
            early_send[0, at : at + SIDE, :] = value[rows - SIDE : rows]
            early_send[1, at : at + SIDE, :] = value[0:SIDE]
            if k < 4:
                coef_win[k, level, main, :] = value
            else:
                total_win[level, main, :] = value

    def exchange(send, recv, send_sem, recv_sem, action):
        def one(side, target):
            return pltpu.make_async_remote_copy(
                src_ref=send.at[side],
                dst_ref=recv.at[side],
                send_sem=send_sem.at[side],
                recv_sem=recv_sem.at[side],
                device_id={"tile": target},
                device_id_type=MESH,
            )

        @pl.when(me < n - 1)
        def _():
            action(0, 1, functools.partial(one, target=me + 1))

        @pl.when(me > 0)
        def _():
            action(1, 0, functools.partial(one, target=me - 1))

    early = (early_send, early_recv, early_send_sem, early_recv_sem)
    late = (late_send, late_recv, late_send_sem, late_recv_sem)
    exchange(*early, lambda out, back, one: one(out).start())

    lat_t[...] = lat[...].astype(jnp.float32).T.astype(jnp.bfloat16)
    loads["weight"].wait()
    loads["innov"].wait()
    edge = jnp.zeros((SIDE, cols), jnp.float32)
    for k in range(STEPS):
        for level in range(levels):
            for target, source in ((weight_win, weight), (innov_win, innov)):
                target[k, level, 0:SIDE, :] = edge
                target[k, level, main, :] = source[k, level]
                target[k, level, SIDE + rows : win, :] = edge

    least, largest = [], []
    for level in range(levels):
        low, high = jnp.int32(n - 1), jnp.int32(0)
        for block in range(n):
            here = level_map[block] == level
            low = jnp.minimum(low, jnp.where(here, block, n - 1))
            high = jnp.maximum(high, jnp.where(here, block, 0))
        least.append(low)
        largest.append(high)

    exchange(*early, lambda out, back, one: one(back).wait_recv())

    @pl.when(me == 0)
    def _():
        early_recv[0] = jnp.zeros(early_recv.shape[1:], jnp.float32)
        late_recv[0] = jnp.zeros(late_recv.shape[1:], jnp.float32)

    @pl.when(me == n - 1)
    def _():
        early_recv[1] = jnp.zeros(early_recv.shape[1:], jnp.float32)
        late_recv[1] = jnp.zeros(late_recv.shape[1:], jnp.float32)

    for level in range(levels):
        for k in range(5):
            at = (k * levels + level) * SIDE
            target = coef_win.at[k, level] if k < 4 else total_win.at[level]
            target[0:SIDE, :] = early_recv[0, at : at + SIDE, :]
            target[SIDE + rows : win, :] = early_recv[1, at : at + SIDE, :]
        keep_win[level] = 1.0 - (
            coef_win[0, level] + coef_win[1, level] + coef_win[2, level] + coef_win[3, level]
        )

    for copy in member_copies:
        copy.wait_recv()

    for level in range(levels):
        state = total_win[level] + (received[least[level]] + received[largest[level]])
        c = [coef_win[k, level] for k in range(4)]
        for k in range(STEPS):
            state = (
                state
                + c[0] * (pltpu.roll(state, win - 1, 0) - state)
                + c[1] * (pltpu.roll(state, 1, 0) - state)
                + c[2] * (pltpu.roll(state, cols - 1, 1) - state)
                + c[3] * (pltpu.roll(state, 1, 1) - state)
            )
            weighted[k, level] = weight_win[k, level] * (state - innov_win[k, level])
        at = level * 8
        for k in range(STEPS):
            first = k * (k + 1) // 2
            late_send[0, at + first : at + first + k + 1, :] = weighted[
                k, level, SIDE + rows - k - 1 : SIDE + rows, :
            ]
            late_send[1, at + first : at + first + k + 1, :] = weighted[
                k, level, SIDE : SIDE + k + 1, :
            ]
    exchange(*late, lambda out, back, one: one(out).start())
    exchange(*late, lambda out, back, one: one(back).wait_recv())
    for level in range(levels):
        at = level * 8
        for k in range(STEPS):
            first = k * (k + 1) // 2
            weighted[k, level, SIDE - k - 1 : SIDE, :] = late_recv[
                0, at + first : at + first + k + 1, :
            ]
            weighted[k, level, SIDE + rows : SIDE + rows + k + 1, :] = late_recv[
                1, at + first : at + first + k + 1, :
            ]
    for level in range(levels):
        adjoint = weighted[STEPS - 1, level]
        c = [coef_win[k, level] for k in range(4)]
        for k in range(STEPS - 2, -2, -1):
            adjoint = (
                keep_win[level] * adjoint
                + pltpu.roll(c[0] * adjoint, 1, 0)
                + pltpu.roll(c[1] * adjoint, win - 1, 0)
                + pltpu.roll(c[2] * adjoint, 1, 1)
                + pltpu.roll(c[3] * adjoint, cols - 1, 1)
            )
            if k >= 0:
                adjoint = adjoint + weighted[k, level]
        grad[level] = adjoint[SIDE : SIDE + rows]

    grad_copies = []
    for d in range(1, n):
        peer = lax.rem(me + d, n)
        grad_send[d] = grad[level_map[peer]]
        copy = pltpu.make_async_remote_copy(
            src_ref=grad_send.at[d],
            dst_ref=grad_field.at[me],
            send_sem=grad_send_sem.at[d],
            recv_sem=grad_recv_sem.at[d],
            device_id={"tile": peer},
            device_id_type=MESH,
        )
        copy.start()
        grad_copies.append(copy)
    grad_field[me] = grad[level_map[me]]

    static_new[...] = static[...] - step_size * (static[...] + scale[...] * grad[...])
    static_store = pltpu.make_async_copy(static_new, static_out, out_sem.at[0])
    static_store.start()

    for copy in member_copies:
        copy.wait_send()
    exchange(*early, lambda out, back, one: one(out).wait_send())
    exchange(*late, lambda out, back, one: one(out).wait_send())
    for copy in grad_copies:
        copy.wait_recv()
    gradient = grad_field[...].reshape(nlat, cols)
    weighted_grad = (perts[...].astype(jnp.float32) * gradient).astype(jnp.bfloat16)
    adjoint_lat = jnp.dot(
        lat_t[...], weighted_grad, preferred_element_type=jnp.float32
    ).astype(jnp.bfloat16)
    member_grad = jnp.dot(adjoint_lat, lon[...], preferred_element_type=jnp.float32)
    ens_new[...] = control[...] - step_size * (control[...] + member_grad)
    ens_store = pltpu.make_async_copy(ens_new, ens_out.at[0], out_sem.at[1])
    ens_store.start()
    for copy in grad_copies:
        copy.wait_send()
    static_store.wait()
    ens_store.wait()


def fused(n, *args):
    level_map, loc_lat, loc_lon, ens_perts, ens_control, static_control = args[:6]
    nlat, cols = ens_control.shape[1:]
    levels, rows, _ = static_control.shape
    win = rows + 2 * SIDE
    f32, bf16 = jnp.float32, jnp.bfloat16
    anywhere = pl.BlockSpec(memory_space=pl.ANY)
    dma = pltpu.SemaphoreType.DMA
    fields = (levels, rows, cols)
    windows = (levels, win, cols)
    return pl.pallas_call(
        functools.partial(kernel, n),
        out_shape=(
            jax.ShapeDtypeStruct(ens_control.shape, f32),
            jax.ShapeDtypeStruct(static_control.shape, f32),
        ),
        in_specs=[pl.BlockSpec(memory_space=pltpu.SMEM)] + [anywhere] * 9,
        out_specs=(anywhere, anywhere),
        scratch_shapes=[
            pltpu.VMEM(loc_lat.shape, bf16),
            pltpu.VMEM(loc_lon.shape, bf16),
            pltpu.VMEM((nlat, cols), bf16),
            pltpu.VMEM((nlat, cols), f32),
            pltpu.VMEM(fields, f32),
            pltpu.VMEM(fields, f32),
            pltpu.VMEM((4,) + fields, f32),
            pltpu.VMEM((STEPS,) + fields, f32),
            pltpu.VMEM((STEPS,) + fields, f32),
            pltpu.VMEM(loc_lat.shape, bf16),
            pltpu.VMEM((nlat + 2 * SIDE, cols), f32),
            pltpu.VMEM((n, win, cols), f32),
            pltpu.VMEM((4,) + windows, f32),
            pltpu.VMEM(windows, f32),
            pltpu.VMEM(windows, f32),
            pltpu.VMEM((STEPS,) + windows, f32),
            pltpu.VMEM((STEPS,) + windows, f32),
            pltpu.VMEM((STEPS,) + windows, f32),
            pltpu.VMEM((2, 5 * levels * SIDE, cols), f32),
            pltpu.VMEM((2, 5 * levels * SIDE, cols), f32),
            pltpu.VMEM((2, levels * 8, cols), f32),
            pltpu.VMEM((2, levels * 8, cols), f32),
            pltpu.VMEM(fields, f32),
            pltpu.VMEM((n, rows, cols), f32),
            pltpu.VMEM((n, rows, cols), f32),
            pltpu.VMEM((nlat, cols), f32),
            pltpu.VMEM(fields, f32),
            dma((9,)),
            dma((2,)),
            dma((n,)),
            dma((n,)),
            dma((2,)),
            dma((2,)),
            dma((2,)),
            dma((2,)),
            dma((n,)),
            dma((n,)),
        ],
        compiler_params=pltpu.CompilerParams(
            collective_id=0, has_side_effects=True, vmem_limit_bytes=48 * 1024 * 1024
        ),
    )(*args)


def device_program(n, *args):
    ens_control, static_control = args[4:6]
    levels, rows, cols = static_control.shape
    fits = (
        ens_control.shape[0] == 1
        and n == 2 * levels
        and rows % 8 == 0
        and rows * n == ens_control.shape[1]
        and cols % 128 == 0
        and STEPS < SIDE
    )
    return fused(n, *args) if fits else local(*args)


def solution(mesh):
    in_specs = (
        P(),
        P(),
        P(),
        P(("groups", "tile"), None, None),
        P(("groups", "tile"), None, None),
        P("groups", "tile", None),
        P("groups", "tile", None),
        P(None, "groups", "tile", None),
        P(None, "groups", "tile", None),
        P(None, "groups", "tile", None),
    )
    out_specs = (P(("groups", "tile"), None, None), P("groups", "tile", None))
    body = functools.partial(device_program, mesh.shape["tile"])
    return jax.shard_map(body, mesh=mesh, in_specs=in_specs, out_specs=out_specs, check_vma=False)
```

```python
import functools

import jax
import jax.numpy as jnp
from jax import lax
from jax.experimental import pallas as pl
from jax.experimental.pallas import tpu as pltpu
from jax.sharding import PartitionSpec as P

STEPS = 3


step_size = 0.15


def extended(block, sides, width):
    for axis, dim in sides:
        count = lax.axis_size(axis)
        forward = [(i, i + 1) for i in range(count - 1)]
        backward = [(target, source) for source, target in forward]
        low = lax.ppermute(
            lax.slice_in_dim(block, block.shape[dim] - width, None, axis=dim), axis, forward
        )
        high = lax.ppermute(lax.slice_in_dim(block, 0, width, axis=dim), axis, backward)
        block = jnp.concatenate([low, block, high], axis=dim)
    return block


def forward_step(state, coeffs):
    padded = extended(state, (("tile", 1),), 1)
    north_rows = padded[:, 2:]
    south_rows = padded[:, :-2]
    east_cells = jnp.roll(state, -1, 2)
    west_cells = jnp.roll(state, 1, 2)
    return (
        state
        + coeffs[0] * (north_rows - state)
        + coeffs[1] * (south_rows - state)
        + coeffs[2] * (east_cells - state)
        + coeffs[3] * (west_cells - state)
    )


def adjoint_step(adjoint, coeffs):
    coef_sum = coeffs[0] + coeffs[1] + coeffs[2] + coeffs[3]
    fluxes = jnp.stack([coeffs[0] * adjoint, coeffs[1] * adjoint])
    padded = extended(fluxes, (("tile", 2),), 1)
    north_flux = padded[0][:, :-2]
    south_flux = padded[1][:, 2:]
    return (
        (1.0 - coef_sum) * adjoint
        + north_flux
        + south_flux
        + jnp.roll(coeffs[2] * adjoint, 1, 2)
        + jnp.roll(coeffs[3] * adjoint, -1, 2)
    )


def window_gradient(total_incr, coefs, obs_weight, innovation):
    state = total_incr
    weighted = []
    for section in range(STEPS):
        state = forward_step(state, coefs)
        weighted.append(obs_weight[section] * (state - innovation[section]))
    adjoint = weighted[STEPS - 1]
    for section in range(STEPS - 2, -1, -1):
        adjoint = adjoint_step(adjoint, coefs) + weighted[section]
    return adjoint_step(adjoint, coefs)


def local(
    level_map,
    loc_lat,
    loc_lon,
    ens_perts,
    ens_control,
    static_control,
    static_scale,
    coefs,
    obs_weight,
    innovation,
):
    tile_count = lax.axis_size("tile")
    my_level = level_map[lax.axis_index("tile")]
    levels = static_control.shape[0]
    level_ids = jnp.arange(levels, dtype=jnp.int32)
    level_onehot = (level_map[:, None] == level_ids[None, :]).astype(jnp.float32)
    control = ens_control
    lat_smoothed = jnp.einsum(
        "ij,bjk->bik", loc_lat, control.astype(jnp.bfloat16), preferred_element_type=jnp.float32
    ).astype(jnp.bfloat16)
    member_field = jnp.einsum(
        "bij,kj->bik", lat_smoothed, loc_lon, preferred_element_type=jnp.float32
    )
    partial_value = jnp.sum(ens_perts.astype(jnp.float32) * member_field, axis=0)
    pieces = partial_value.reshape(tile_count, -1, partial_value.shape[1])
    received = lax.all_to_all(pieces, "tile", split_axis=0, concat_axis=0, tiled=True)
    ens_incr = jnp.einsum("dl,dij->lij", level_onehot, received, precision=lax.Precision.HIGHEST)
    total_incr = static_scale * static_control + ens_incr
    gradient = window_gradient(total_incr, coefs, obs_weight, innovation)
    static_control = static_control - step_size * (static_control + static_scale * gradient)
    gathered = lax.all_gather(gradient, "tile", axis=1, tiled=True)
    grad_field = lax.dynamic_index_in_dim(gathered, my_level, 0, keepdims=False)
    weighted_grad = (ens_perts.astype(jnp.float32) * grad_field[None]).astype(jnp.bfloat16)
    adjoint_lat = jnp.einsum(
        "ji,bjk->bik", loc_lat, weighted_grad, preferred_element_type=jnp.float32
    ).astype(jnp.bfloat16)
    member_grad = jnp.einsum(
        "bij,jk->bik", adjoint_lat, loc_lon, preferred_element_type=jnp.float32
    )
    control = control - step_size * (control + member_grad)
    return (control, static_control)


MESH = pl.DeviceIdType.MESH
SIDE = 4


def kernel(
    n,
    level_hbm,
    lat_hbm,
    lon_hbm,
    perts_hbm,
    control_hbm,
    static_hbm,
    scale_hbm,
    coefs_hbm,
    weight_hbm,
    innov_hbm,
    ens_out,
    static_out,
    level_map,
    blocks_of,
    lat,
    lon,
    perts,
    control,
    static,
    scale,
    coefs,
    weight,
    innov,
    lat_t,
    field,
    received,
    coef_win,
    keep_win,
    total_win,
    weight_win,
    innov_win,
    weighted,
    early_send,
    early_recv,
    late_send,
    late_recv,
    grad,
    grad_send,
    grad_field,
    ens_new,
    static_new,
    in_sem,
    out_sem,
    member_send_sem,
    member_recv_sem,
    early_send_sem,
    early_recv_sem,
    late_send_sem,
    late_recv_sem,
    grad_send_sem,
    grad_recv_sem,
):
    me = lax.axis_index("tile")
    levels, rows, cols = static.shape
    nlat = control.shape[0]
    win = rows + 2 * SIDE
    main = slice(SIDE, SIDE + rows)

    def each_level(body):
        def two(pair, carry):
            for half in range(2):
                body(pair, half, 2 * pair + half)
            return carry

        lax.fori_loop(0, levels // 2, two, 0)

    loads = {}
    for place, (name, source, target) in enumerate(
        (
            ("control", control_hbm.at[0], control),
            ("lat", lat_hbm, lat),
            ("lon", lon_hbm, lon),
            ("perts", perts_hbm.at[0], perts),
            ("coefs", coefs_hbm, coefs),
            ("static", static_hbm, static),
            ("scale", scale_hbm, scale),
            ("weight", weight_hbm, weight),
            ("innov", innov_hbm, innov),
        )
    ):
        loads[name] = pltpu.make_async_copy(source, target, in_sem.at[place])
        loads[name].start()
    level_load = pltpu.make_async_copy(level_hbm, level_map, out_sem.at[2])
    level_load.start()

    barrier = pltpu.get_barrier_semaphore()
    for d in range(1, n):
        pl.semaphore_signal(
            barrier, inc=1, device_id={"tile": lax.rem(me + d, n)}, device_id_type=MESH
        )

    loads["control"].wait()
    loads["lat"].wait()
    smoothed = jnp.dot(
        lat[...], control[...].astype(jnp.bfloat16), preferred_element_type=jnp.float32
    ).astype(jnp.bfloat16)
    loads["lon"].wait()
    member = lax.dot_general(
        smoothed, lon[...], (((1,), (1,)), ((), ())), preferred_element_type=jnp.float32
    )
    loads["perts"].wait()
    field[0:SIDE, :] = jnp.zeros((SIDE, cols), jnp.float32)
    field[SIDE + nlat : 2 * SIDE + nlat, :] = jnp.zeros((SIDE, cols), jnp.float32)
    field[SIDE : SIDE + nlat, :] = perts[...].astype(jnp.float32) * member

    pl.semaphore_wait(barrier, n - 1)

    def window(tile):
        return pl.ds(pl.multiple_of(tile * rows, 8), win)

    order = sorted(range(1, n), key=lambda d: abs(2 * d - n))
    member_copies = []
    for d in order:
        peer = lax.rem(me + d, n)
        copy = pltpu.make_async_remote_copy(
            src_ref=field.at[window(peer)],
            dst_ref=received.at[me],
            send_sem=member_send_sem.at[d],
            recv_sem=member_recv_sem.at[d],
            device_id={"tile": peer},
            device_id_type=MESH,
        )
        copy.start()
        member_copies.append(copy)
    received[me] = field[window(me), :]

    loads["coefs"].wait()
    loads["static"].wait()
    loads["scale"].wait()

    def early_rows(pair, half, level):
        for k in range(4):
            early_send[0, level, 2 * k : 2 * k + 2, :] = coefs[k, level, rows - 2 : rows, :]
            early_send[1, level, 2 * k : 2 * k + 2, :] = coefs[k, level, 0:2, :]
            coef_win[k, level, main, :] = coefs[k, level]
        value = scale[level] * static[level]
        at = half * SIDE
        early_send[0, levels + pair, at : at + SIDE, :] = value[rows - SIDE : rows]
        early_send[1, levels + pair, at : at + SIDE, :] = value[0:SIDE]
        total_win[level, main, :] = value

    each_level(early_rows)

    def exchange(send, recv, send_sem, recv_sem, action):
        def one(side, target):
            return pltpu.make_async_remote_copy(
                src_ref=send.at[side],
                dst_ref=recv.at[side],
                send_sem=send_sem.at[side],
                recv_sem=recv_sem.at[side],
                device_id={"tile": target},
                device_id_type=MESH,
            )

        @pl.when(me < n - 1)
        def _():
            action(0, 1, functools.partial(one, target=me + 1))

        @pl.when(me > 0)
        def _():
            action(1, 0, functools.partial(one, target=me - 1))

    early = (early_send, early_recv, early_send_sem, early_recv_sem)
    late = (late_send, late_recv, late_send_sem, late_recv_sem)
    exchange(*early, lambda out, back, one: one(out).start())

    lat_t[...] = lat[...].astype(jnp.float32).T.astype(jnp.bfloat16)
    loads["weight"].wait()
    loads["innov"].wait()
    edge = jnp.zeros((SIDE, cols), jnp.float32)

    def widen(pair, half, level):
        for k in range(STEPS):
            for target, source in ((weight_win, weight), (innov_win, innov)):
                target[k, level, 0:SIDE, :] = edge
                target[k, level, main, :] = source[k, level]
                target[k, level, SIDE + rows : win, :] = edge

    each_level(widen)

    level_load.wait()

    def find(level, carry):
        low, high = jnp.int32(n - 1), jnp.int32(0)
        for block in range(n):
            here = level_map[block] == level
            low = jnp.minimum(low, jnp.where(here, block, n - 1))
            high = jnp.maximum(high, jnp.where(here, block, 0))
        blocks_of[0, level] = low
        blocks_of[1, level] = high
        return carry

    lax.fori_loop(0, levels, find, 0)

    exchange(*early, lambda out, back, one: one(back).wait_recv())

    @pl.when(me == 0)
    def _():
        early_recv[0] = jnp.zeros(early_recv.shape[1:], jnp.float32)
        late_recv[0] = jnp.zeros(late_recv.shape[1:], jnp.float32)

    @pl.when(me == n - 1)
    def _():
        early_recv[1] = jnp.zeros(early_recv.shape[1:], jnp.float32)
        late_recv[1] = jnp.zeros(late_recv.shape[1:], jnp.float32)

    def unpack_early(pair, half, level):
        at = half * SIDE
        for k in range(4):
            coef_win[k, level, 0 : SIDE - 2, :] = jnp.full(
                (SIDE - 2, cols), 1.0 if k == 0 else 0.0, jnp.float32
            )
            coef_win[k, level, SIDE - 2 : SIDE, :] = early_recv[0, level, 2 * k : 2 * k + 2, :]
            coef_win[k, level, SIDE + rows : SIDE + rows + 2, :] = early_recv[
                1, level, 2 * k : 2 * k + 2, :
            ]
            coef_win[k, level, SIDE + rows + 2 : win, :] = jnp.full(
                (SIDE - 2, cols), 1.0 if k == 1 else 0.0, jnp.float32
            )
        total_win[level, 0:SIDE, :] = early_recv[0, levels + pair, at : at + SIDE, :]
        total_win[level, SIDE + rows : win, :] = early_recv[1, levels + pair, at : at + SIDE, :]
        keep_win[level] = 1.0 - (
            coef_win[0, level] + coef_win[1, level] + coef_win[2, level] + coef_win[3, level]
        )

    each_level(unpack_early)

    for copy in member_copies:
        copy.wait_recv()

    def forward(pair, half, level):
        state = total_win[level] + (received[blocks_of[0, level]] + received[blocks_of[1, level]])
        c = [coef_win[k, level] for k in range(4)]
        for k in range(STEPS):
            state = (
                state
                + c[0] * (pltpu.roll(state, win - 1, 0) - state)
                + c[1] * (pltpu.roll(state, 1, 0) - state)
                + c[2] * (pltpu.roll(state, cols - 1, 1) - state)
                + c[3] * (pltpu.roll(state, 1, 1) - state)
            )
            value = weight_win[k, level] * (state - innov_win[k, level])
            weighted[k, level] = value
            at = k * (k + 1) // 2
            low, high = SIDE, SIDE + rows
            near = min(k + 1, 2)
            late_send[0, level, at : at + near, :] = value[high - near : high]
            late_send[1, level, at : at + near, :] = value[low : low + near]
            if k == 2:
                late_send[0, level, at + 2 : at + 3, :] = (c[0] * value)[high - 3 : high - 2]
                late_send[1, level, at + 2 : at + 3, :] = (c[1] * value)[low + 2 : low + 3]

    each_level(forward)
    exchange(*late, lambda out, back, one: one(out).start())
    exchange(*late, lambda out, back, one: one(back).wait_recv())

    def backward(pair, half, level):
        for k in range(STEPS):
            at = k * (k + 1) // 2
            low, high = SIDE, SIDE + rows
            near = min(k + 1, 2)
            weighted[k, level, low - near : low, :] = late_recv[0, level, at : at + near, :]
            weighted[k, level, high : high + near, :] = late_recv[1, level, at : at + near, :]
            if k == 2:
                weighted[k, level, low - 3 : low - 2, :] = late_recv[0, level, at + 2 : at + 3, :]
                weighted[k, level, high + 2 : high + 3, :] = late_recv[
                    1, level, at + 2 : at + 3, :
                ]
        adjoint = weighted[STEPS - 1, level]
        c = [coef_win[k, level] for k in range(4)]
        for k in range(STEPS - 2, -2, -1):
            adjoint = (
                keep_win[level] * adjoint
                + pltpu.roll(c[0] * adjoint, 1, 0)
                + pltpu.roll(c[1] * adjoint, win - 1, 0)
                + pltpu.roll(c[2] * adjoint, 1, 1)
                + pltpu.roll(c[3] * adjoint, cols - 1, 1)
            )
            if k >= 0:
                adjoint = adjoint + weighted[k, level]
        grad[level] = adjoint[SIDE : SIDE + rows]

    each_level(backward)

    grad_copies = []
    for d in order:
        peer = lax.rem(me + d, n)
        grad_send[d] = grad[level_map[peer]]
        copy = pltpu.make_async_remote_copy(
            src_ref=grad_send.at[d],
            dst_ref=grad_field.at[me],
            send_sem=grad_send_sem.at[d],
            recv_sem=grad_recv_sem.at[d],
            device_id={"tile": peer},
            device_id_type=MESH,
        )
        copy.start()
        grad_copies.append(copy)
    grad_field[me] = grad[level_map[me]]

    static_new[...] = static[...] - step_size * (static[...] + scale[...] * grad[...])
    static_store = pltpu.make_async_copy(static_new, static_out, out_sem.at[0])
    static_store.start()

    for copy in member_copies:
        copy.wait_send()
    exchange(*early, lambda out, back, one: one(out).wait_send())
    exchange(*late, lambda out, back, one: one(out).wait_send())
    for copy in grad_copies:
        copy.wait_recv()
    gradient = grad_field[...].reshape(nlat, cols)
    weighted_grad = (perts[...].astype(jnp.float32) * gradient).astype(jnp.bfloat16)
    adjoint_lat = jnp.dot(
        lat_t[...], weighted_grad, preferred_element_type=jnp.float32
    ).astype(jnp.bfloat16)
    member_grad = jnp.dot(adjoint_lat, lon[...], preferred_element_type=jnp.float32)
    ens_new[...] = control[...] - step_size * (control[...] + member_grad)
    ens_store = pltpu.make_async_copy(ens_new, ens_out.at[0], out_sem.at[1])
    ens_store.start()
    for copy in grad_copies:
        copy.wait_send()
    static_store.wait()
    ens_store.wait()


def fused(n, *args):
    level_map, loc_lat, loc_lon, ens_perts, ens_control, static_control = args[:6]
    nlat, cols = ens_control.shape[1:]
    levels, rows, _ = static_control.shape
    win = rows + 2 * SIDE
    f32, bf16 = jnp.float32, jnp.bfloat16
    anywhere = pl.BlockSpec(memory_space=pl.ANY)
    dma = pltpu.SemaphoreType.DMA
    fields = (levels, rows, cols)
    windows = (levels, win, cols)
    return pl.pallas_call(
        functools.partial(kernel, n),
        out_shape=(
            jax.ShapeDtypeStruct(ens_control.shape, f32),
            jax.ShapeDtypeStruct(static_control.shape, f32),
        ),
        in_specs=[pl.BlockSpec(memory_space=pltpu.HBM)] * 10,
        out_specs=(anywhere, anywhere),
        scratch_shapes=[
            pltpu.SMEM(level_map.shape, jnp.int32),
            pltpu.SMEM((2, levels), jnp.int32),
            pltpu.VMEM(loc_lat.shape, bf16),
            pltpu.VMEM(loc_lon.shape, bf16),
            pltpu.VMEM((nlat, cols), bf16),
            pltpu.VMEM((nlat, cols), f32),
            pltpu.VMEM(fields, f32),
            pltpu.VMEM(fields, f32),
            pltpu.VMEM((4,) + fields, f32),
            pltpu.VMEM((STEPS,) + fields, f32),
            pltpu.VMEM((STEPS,) + fields, f32),
            pltpu.VMEM(loc_lat.shape, bf16),
            pltpu.VMEM((nlat + 2 * SIDE, cols), f32),
            pltpu.VMEM((n, win, cols), f32),
            pltpu.VMEM((4,) + windows, f32),
            pltpu.VMEM(windows, f32),
            pltpu.VMEM(windows, f32),
            pltpu.VMEM((STEPS,) + windows, f32),
            pltpu.VMEM((STEPS,) + windows, f32),
            pltpu.VMEM((STEPS,) + windows, f32),
            pltpu.VMEM((2, levels + levels // 2, 8, cols), f32),
            pltpu.VMEM((2, levels + levels // 2, 8, cols), f32),
            pltpu.VMEM((2, levels, 8, cols), f32),
            pltpu.VMEM((2, levels, 8, cols), f32),
            pltpu.VMEM(fields, f32),
            pltpu.VMEM((n, rows, cols), f32),
            pltpu.VMEM((n, rows, cols), f32),
            pltpu.VMEM((nlat, cols), f32),
            pltpu.VMEM(fields, f32),
            dma((9,)),
            dma((3,)),
            dma((n,)),
            dma((n,)),
            dma((2,)),
            dma((2,)),
            dma((2,)),
            dma((2,)),
            dma((n,)),
            dma((n,)),
        ],
        compiler_params=pltpu.CompilerParams(
            collective_id=0, has_side_effects=True, vmem_limit_bytes=48 * 1024 * 1024
        ),
    )(*args)


def device_program(n, *args):
    ens_control, static_control = args[4:6]
    levels, rows, cols = static_control.shape
    fits = (
        ens_control.shape[0] == 1
        and n == 2 * levels
        and rows % 8 == 0
        and rows * n == ens_control.shape[1]
        and cols % 128 == 0
        and levels % 2 == 0
        and STEPS == 3
    )
    return fused(n, *args) if fits else local(*args)


def solution(mesh):
    in_specs = (
        P(),
        P(),
        P(),
        P(("groups", "tile"), None, None),
        P(("groups", "tile"), None, None),
        P("groups", "tile", None),
        P("groups", "tile", None),
        P(None, "groups", "tile", None),
        P(None, "groups", "tile", None),
        P(None, "groups", "tile", None),
    )
    out_specs = (P(("groups", "tile"), None, None), P("groups", "tile", None))
    body = functools.partial(device_program, mesh.shape["tile"])
    return jax.shard_map(body, mesh=mesh, in_specs=in_specs, out_specs=out_specs, check_vma=False)
```

```python
import functools

import jax
import jax.numpy as jnp
from jax import lax
from jax.experimental import pallas as pl
from jax.experimental.pallas import tpu as pltpu
from jax.sharding import PartitionSpec as P

STEPS = 3


step_size = 0.15


def extended(block, sides, width):
    for axis, dim in sides:
        count = lax.axis_size(axis)
        forward = [(i, i + 1) for i in range(count - 1)]
        backward = [(target, source) for source, target in forward]
        low = lax.ppermute(
            lax.slice_in_dim(block, block.shape[dim] - width, None, axis=dim), axis, forward
        )
        high = lax.ppermute(lax.slice_in_dim(block, 0, width, axis=dim), axis, backward)
        block = jnp.concatenate([low, block, high], axis=dim)
    return block


def forward_step(state, coeffs):
    padded = extended(state, (("tile", 1),), 1)
    north_rows = padded[:, 2:]
    south_rows = padded[:, :-2]
    east_cells = jnp.roll(state, -1, 2)
    west_cells = jnp.roll(state, 1, 2)
    return (
        state
        + coeffs[0] * (north_rows - state)
        + coeffs[1] * (south_rows - state)
        + coeffs[2] * (east_cells - state)
        + coeffs[3] * (west_cells - state)
    )


def adjoint_step(adjoint, coeffs):
    coef_sum = coeffs[0] + coeffs[1] + coeffs[2] + coeffs[3]
    fluxes = jnp.stack([coeffs[0] * adjoint, coeffs[1] * adjoint])
    padded = extended(fluxes, (("tile", 2),), 1)
    north_flux = padded[0][:, :-2]
    south_flux = padded[1][:, 2:]
    return (
        (1.0 - coef_sum) * adjoint
        + north_flux
        + south_flux
        + jnp.roll(coeffs[2] * adjoint, 1, 2)
        + jnp.roll(coeffs[3] * adjoint, -1, 2)
    )


def window_gradient(total_incr, coefs, obs_weight, innovation):
    state = total_incr
    weighted = []
    for section in range(STEPS):
        state = forward_step(state, coefs)
        weighted.append(obs_weight[section] * (state - innovation[section]))
    adjoint = weighted[STEPS - 1]
    for section in range(STEPS - 2, -1, -1):
        adjoint = adjoint_step(adjoint, coefs) + weighted[section]
    return adjoint_step(adjoint, coefs)


def local(
    level_map,
    loc_lat,
    loc_lon,
    ens_perts,
    ens_control,
    static_control,
    static_scale,
    coefs,
    obs_weight,
    innovation,
):
    tile_count = lax.axis_size("tile")
    my_level = level_map[lax.axis_index("tile")]
    levels = static_control.shape[0]
    level_ids = jnp.arange(levels, dtype=jnp.int32)
    level_onehot = (level_map[:, None] == level_ids[None, :]).astype(jnp.float32)
    control = ens_control
    lat_smoothed = jnp.einsum(
        "ij,bjk->bik", loc_lat, control.astype(jnp.bfloat16), preferred_element_type=jnp.float32
    ).astype(jnp.bfloat16)
    member_field = jnp.einsum(
        "bij,kj->bik", lat_smoothed, loc_lon, preferred_element_type=jnp.float32
    )
    partial_value = jnp.sum(ens_perts.astype(jnp.float32) * member_field, axis=0)
    pieces = partial_value.reshape(tile_count, -1, partial_value.shape[1])
    received = lax.all_to_all(pieces, "tile", split_axis=0, concat_axis=0, tiled=True)
    ens_incr = jnp.einsum("dl,dij->lij", level_onehot, received, precision=lax.Precision.HIGHEST)
    total_incr = static_scale * static_control + ens_incr
    gradient = window_gradient(total_incr, coefs, obs_weight, innovation)
    static_control = static_control - step_size * (static_control + static_scale * gradient)
    gathered = lax.all_gather(gradient, "tile", axis=1, tiled=True)
    grad_field = lax.dynamic_index_in_dim(gathered, my_level, 0, keepdims=False)
    weighted_grad = (ens_perts.astype(jnp.float32) * grad_field[None]).astype(jnp.bfloat16)
    adjoint_lat = jnp.einsum(
        "ji,bjk->bik", loc_lat, weighted_grad, preferred_element_type=jnp.float32
    ).astype(jnp.bfloat16)
    member_grad = jnp.einsum(
        "bij,jk->bik", adjoint_lat, loc_lon, preferred_element_type=jnp.float32
    )
    control = control - step_size * (control + member_grad)
    return (control, static_control)


MESH = pl.DeviceIdType.MESH
SIDE = 4


def kernel(
    n,
    level_hbm,
    lat_hbm,
    lon_hbm,
    perts_hbm,
    control_hbm,
    static_hbm,
    scale_hbm,
    coefs_hbm,
    weight_hbm,
    innov_hbm,
    ens_out,
    static_out,
    level_map,
    blocks_of,
    lat,
    lon,
    perts,
    control,
    static,
    scale,
    coefs,
    weight,
    innov,
    lat_t,
    field,
    received,
    coef_win,
    keep_win,
    total_win,
    weight_win,
    innov_win,
    weighted,
    early_send,
    early_recv,
    late_send,
    late_recv,
    grad,
    grad_send,
    grad_field,
    ens_new,
    static_new,
    in_sem,
    out_sem,
    member_send_sem,
    member_recv_sem,
    early_send_sem,
    early_recv_sem,
    late_send_sem,
    late_recv_sem,
    grad_send_sem,
    grad_recv_sem,
):
    me = lax.axis_index("tile")
    levels, rows, cols = static.shape
    nlat = control.shape[0]
    win = rows + 2 * SIDE
    main = slice(SIDE, SIDE + rows)

    def each_level(body, before=None, after=None):
        def two(pair, carry):
            if before is not None:
                before(pair)
            for half in range(2):
                body(pair, half, 2 * pair + half)
            if after is not None:
                after(pair)
            return carry

        lax.fori_loop(0, levels // 2, two, 0)

    loads = {}
    for place, (name, source, target) in enumerate(
        (
            ("control", control_hbm.at[0], control),
            ("lat", lat_hbm, lat),
            ("lon", lon_hbm, lon),
            ("perts", perts_hbm.at[0], perts),
            ("coefs", coefs_hbm, coefs),
            ("static", static_hbm, static),
            ("scale", scale_hbm, scale),
            ("weight", weight_hbm, weight),
            ("innov", innov_hbm, innov),
        )
    ):
        loads[name] = pltpu.make_async_copy(source, target, in_sem.at[place])
        loads[name].start()
    level_load = pltpu.make_async_copy(level_hbm, level_map, out_sem.at[2])
    level_load.start()

    barrier = pltpu.get_barrier_semaphore()
    for d in range(1, n):
        pl.semaphore_signal(
            barrier, inc=1, device_id={"tile": lax.rem(me + d, n)}, device_id_type=MESH
        )

    loads["control"].wait()
    loads["lat"].wait()
    smoothed = jnp.dot(
        lat[...], control[...].astype(jnp.bfloat16), preferred_element_type=jnp.float32
    ).astype(jnp.bfloat16)
    loads["lon"].wait()
    member = lax.dot_general(
        smoothed, lon[...], (((1,), (1,)), ((), ())), preferred_element_type=jnp.float32
    )
    loads["perts"].wait()
    field[0:SIDE, :] = jnp.zeros((SIDE, cols), jnp.float32)
    field[SIDE + nlat : 2 * SIDE + nlat, :] = jnp.zeros((SIDE, cols), jnp.float32)
    field[SIDE : SIDE + nlat, :] = perts[...].astype(jnp.float32) * member

    pl.semaphore_wait(barrier, n - 1)

    def window(tile):
        return pl.ds(pl.multiple_of(tile * rows, 8), win)

    order = sorted(range(1, n), key=lambda d: abs(2 * d - n))
    member_copies = []
    for d in order:
        peer = lax.rem(me + d, n)
        copy = pltpu.make_async_remote_copy(
            src_ref=field.at[window(peer)],
            dst_ref=received.at[me],
            send_sem=member_send_sem.at[d],
            recv_sem=member_recv_sem.at[d],
            device_id={"tile": peer},
            device_id_type=MESH,
        )
        copy.start()
        member_copies.append(copy)
    received[me] = field[window(me), :]

    loads["coefs"].wait()
    loads["static"].wait()
    loads["scale"].wait()

    def early_rows(pair, half, level):
        for k in range(4):
            early_send[0, level, 2 * k : 2 * k + 2, :] = coefs[k, level, rows - 2 : rows, :]
            early_send[1, level, 2 * k : 2 * k + 2, :] = coefs[k, level, 0:2, :]
            coef_win[k, level, main, :] = coefs[k, level]
        value = scale[level] * static[level]
        at = half * SIDE
        early_send[0, levels + pair, at : at + SIDE, :] = value[rows - SIDE : rows]
        early_send[1, levels + pair, at : at + SIDE, :] = value[0:SIDE]
        total_win[level, main, :] = value

    each_level(early_rows)

    def exchange(send, recv, send_sem, recv_sem, action, chunk=0, width=None):
        def one(side, target):
            part = (side,) if width is None else (side, pl.ds(chunk * width, width))
            return pltpu.make_async_remote_copy(
                src_ref=send.at[part],
                dst_ref=recv.at[part],
                send_sem=send_sem.at[side, chunk],
                recv_sem=recv_sem.at[side, chunk],
                device_id={"tile": target},
                device_id_type=MESH,
            )

        @pl.when(me < n - 1)
        def _():
            action(0, 1, functools.partial(one, target=me + 1))

        @pl.when(me > 0)
        def _():
            action(1, 0, functools.partial(one, target=me - 1))

    def start(out, back, one):
        one(out).start()

    def wait_recv(out, back, one):
        one(back).wait_recv()

    def wait_send(out, back, one):
        one(out).wait_send()

    early = (early_send, early_recv, early_send_sem, early_recv_sem)
    late = (late_send, late_recv, late_send_sem, late_recv_sem)
    exchange(*early, start)

    lat_t[...] = lat[...].astype(jnp.float32).T.astype(jnp.bfloat16)
    loads["weight"].wait()
    loads["innov"].wait()
    edge = jnp.zeros((SIDE, cols), jnp.float32)

    def widen(pair, half, level):
        for k in range(STEPS):
            for target, source in ((weight_win, weight), (innov_win, innov)):
                target[k, level, 0:SIDE, :] = edge
                target[k, level, main, :] = source[k, level]
                target[k, level, SIDE + rows : win, :] = edge

    each_level(widen)

    level_load.wait()

    def find(level, carry):
        low, high = jnp.int32(n - 1), jnp.int32(0)
        for block in range(n):
            here = level_map[block] == level
            low = jnp.minimum(low, jnp.where(here, block, n - 1))
            high = jnp.maximum(high, jnp.where(here, block, 0))
        blocks_of[0, level] = low
        blocks_of[1, level] = high
        return carry

    lax.fori_loop(0, levels, find, 0)

    exchange(*early, wait_recv)

    @pl.when(me == 0)
    def _():
        early_recv[0] = jnp.zeros(early_recv.shape[1:], jnp.float32)
        late_recv[0] = jnp.zeros(late_recv.shape[1:], jnp.float32)

    @pl.when(me == n - 1)
    def _():
        early_recv[1] = jnp.zeros(early_recv.shape[1:], jnp.float32)
        late_recv[1] = jnp.zeros(late_recv.shape[1:], jnp.float32)

    def unpack_early(pair, half, level):
        at = half * SIDE
        for k in range(4):
            coef_win[k, level, 0 : SIDE - 2, :] = jnp.full(
                (SIDE - 2, cols), 1.0 if k == 0 else 0.0, jnp.float32
            )
            coef_win[k, level, SIDE - 2 : SIDE, :] = early_recv[0, level, 2 * k : 2 * k + 2, :]
            coef_win[k, level, SIDE + rows : SIDE + rows + 2, :] = early_recv[
                1, level, 2 * k : 2 * k + 2, :
            ]
            coef_win[k, level, SIDE + rows + 2 : win, :] = jnp.full(
                (SIDE - 2, cols), 1.0 if k == 1 else 0.0, jnp.float32
            )
        total_win[level, 0:SIDE, :] = early_recv[0, levels + pair, at : at + SIDE, :]
        total_win[level, SIDE + rows : win, :] = early_recv[1, levels + pair, at : at + SIDE, :]
        keep_win[level] = 1.0 - (
            coef_win[0, level] + coef_win[1, level] + coef_win[2, level] + coef_win[3, level]
        )

    each_level(unpack_early)

    for copy in member_copies:
        copy.wait_recv()

    def forward(pair, half, level):
        state = total_win[level] + (received[blocks_of[0, level]] + received[blocks_of[1, level]])
        c = [coef_win[k, level] for k in range(4)]
        for k in range(STEPS):
            state = (
                state
                + c[0] * (pltpu.roll(state, win - 1, 0) - state)
                + c[1] * (pltpu.roll(state, 1, 0) - state)
                + c[2] * (pltpu.roll(state, cols - 1, 1) - state)
                + c[3] * (pltpu.roll(state, 1, 1) - state)
            )
            value = weight_win[k, level] * (state - innov_win[k, level])
            weighted[k, level] = value
            at = k * (k + 1) // 2
            low, high = SIDE, SIDE + rows
            near = min(k + 1, 2)
            late_send[0, level, at : at + near, :] = value[high - near : high]
            late_send[1, level, at : at + near, :] = value[low : low + near]
            if k == 2:
                late_send[0, level, at + 2 : at + 3, :] = (c[0] * value)[high - 3 : high - 2]
                late_send[1, level, at + 2 : at + 3, :] = (c[1] * value)[low + 2 : low + 3]

    each_level(forward, after=lambda pair: exchange(*late, start, pair, 2))

    def backward(pair, half, level):
        for k in range(STEPS):
            at = k * (k + 1) // 2
            low, high = SIDE, SIDE + rows
            near = min(k + 1, 2)
            weighted[k, level, low - near : low, :] = late_recv[0, level, at : at + near, :]
            weighted[k, level, high : high + near, :] = late_recv[1, level, at : at + near, :]
            if k == 2:
                weighted[k, level, low - 3 : low - 2, :] = late_recv[0, level, at + 2 : at + 3, :]
                weighted[k, level, high + 2 : high + 3, :] = late_recv[
                    1, level, at + 2 : at + 3, :
                ]
        adjoint = weighted[STEPS - 1, level]
        c = [coef_win[k, level] for k in range(4)]
        for k in range(STEPS - 2, -2, -1):
            adjoint = (
                keep_win[level] * adjoint
                + pltpu.roll(c[0] * adjoint, 1, 0)
                + pltpu.roll(c[1] * adjoint, win - 1, 0)
                + pltpu.roll(c[2] * adjoint, 1, 1)
                + pltpu.roll(c[3] * adjoint, cols - 1, 1)
            )
            if k >= 0:
                adjoint = adjoint + weighted[k, level]
        grad[level] = adjoint[SIDE : SIDE + rows]

    each_level(backward, before=lambda pair: exchange(*late, wait_recv, pair, 2))

    grad_copies = []
    for d in order:
        peer = lax.rem(me + d, n)
        grad_send[d] = grad[level_map[peer]]
        copy = pltpu.make_async_remote_copy(
            src_ref=grad_send.at[d],
            dst_ref=grad_field.at[me],
            send_sem=grad_send_sem.at[d],
            recv_sem=grad_recv_sem.at[d],
            device_id={"tile": peer},
            device_id_type=MESH,
        )
        copy.start()
        grad_copies.append(copy)
    grad_field[me] = grad[level_map[me]]

    static_new[...] = static[...] - step_size * (static[...] + scale[...] * grad[...])
    static_store = pltpu.make_async_copy(static_new, static_out, out_sem.at[0])
    static_store.start()

    for copy in member_copies:
        copy.wait_send()
    exchange(*early, wait_send)
    each_level(lambda *_: None, before=lambda pair: exchange(*late, wait_send, pair, 2))
    for copy in grad_copies:
        copy.wait_recv()
    gradient = grad_field[...].reshape(nlat, cols)
    weighted_grad = (perts[...].astype(jnp.float32) * gradient).astype(jnp.bfloat16)
    adjoint_lat = jnp.dot(
        lat_t[...], weighted_grad, preferred_element_type=jnp.float32
    ).astype(jnp.bfloat16)
    member_grad = jnp.dot(adjoint_lat, lon[...], preferred_element_type=jnp.float32)
    ens_new[...] = control[...] - step_size * (control[...] + member_grad)
    ens_store = pltpu.make_async_copy(ens_new, ens_out.at[0], out_sem.at[1])
    ens_store.start()
    for copy in grad_copies:
        copy.wait_send()
    static_store.wait()
    ens_store.wait()


def fused(n, *args):
    level_map, loc_lat, loc_lon, ens_perts, ens_control, static_control = args[:6]
    nlat, cols = ens_control.shape[1:]
    levels, rows, _ = static_control.shape
    win = rows + 2 * SIDE
    f32, bf16 = jnp.float32, jnp.bfloat16
    anywhere = pl.BlockSpec(memory_space=pl.ANY)
    dma = pltpu.SemaphoreType.DMA
    fields = (levels, rows, cols)
    windows = (levels, win, cols)
    return pl.pallas_call(
        functools.partial(kernel, n),
        out_shape=(
            jax.ShapeDtypeStruct(ens_control.shape, f32),
            jax.ShapeDtypeStruct(static_control.shape, f32),
        ),
        in_specs=[pl.BlockSpec(memory_space=pltpu.HBM)] * 10,
        out_specs=(anywhere, anywhere),
        scratch_shapes=[
            pltpu.SMEM(level_map.shape, jnp.int32),
            pltpu.SMEM((2, levels), jnp.int32),
            pltpu.VMEM(loc_lat.shape, bf16),
            pltpu.VMEM(loc_lon.shape, bf16),
            pltpu.VMEM((nlat, cols), bf16),
            pltpu.VMEM((nlat, cols), f32),
            pltpu.VMEM(fields, f32),
            pltpu.VMEM(fields, f32),
            pltpu.VMEM((4,) + fields, f32),
            pltpu.VMEM((STEPS,) + fields, f32),
            pltpu.VMEM((STEPS,) + fields, f32),
            pltpu.VMEM(loc_lat.shape, bf16),
            pltpu.VMEM((nlat + 2 * SIDE, cols), f32),
            pltpu.VMEM((n, win, cols), f32),
            pltpu.VMEM((4,) + windows, f32),
            pltpu.VMEM(windows, f32),
            pltpu.VMEM(windows, f32),
            pltpu.VMEM((STEPS,) + windows, f32),
            pltpu.VMEM((STEPS,) + windows, f32),
            pltpu.VMEM((STEPS,) + windows, f32),
            pltpu.VMEM((2, levels + levels // 2, 8, cols), f32),
            pltpu.VMEM((2, levels + levels // 2, 8, cols), f32),
            pltpu.VMEM((2, levels, 8, cols), f32),
            pltpu.VMEM((2, levels, 8, cols), f32),
            pltpu.VMEM(fields, f32),
            pltpu.VMEM((n, rows, cols), f32),
            pltpu.VMEM((n, rows, cols), f32),
            pltpu.VMEM((nlat, cols), f32),
            pltpu.VMEM(fields, f32),
            dma((9,)),
            dma((3,)),
            dma((n,)),
            dma((n,)),
            dma((2, 1)),
            dma((2, 1)),
            dma((2, levels // 2)),
            dma((2, levels // 2)),
            dma((n,)),
            dma((n,)),
        ],
        compiler_params=pltpu.CompilerParams(
            collective_id=0, has_side_effects=True
        ),
    )(*args)


def device_program(n, *args):
    ens_control, static_control = args[4:6]
    levels, rows, cols = static_control.shape
    fits = (
        ens_control.shape[0] == 1
        and n == 2 * levels
        and rows % 8 == 0
        and rows * n == ens_control.shape[1]
        and cols % 128 == 0
        and levels % 2 == 0
        and STEPS == 3
    )
    return fused(n, *args) if fits else local(*args)


def solution(mesh):
    in_specs = (
        P(),
        P(),
        P(),
        P(("groups", "tile"), None, None),
        P(("groups", "tile"), None, None),
        P("groups", "tile", None),
        P("groups", "tile", None),
        P(None, "groups", "tile", None),
        P(None, "groups", "tile", None),
        P(None, "groups", "tile", None),
    )
    out_specs = (P(("groups", "tile"), None, None), P("groups", "tile", None))
    body = functools.partial(device_program, mesh.shape["tile"])
    return jax.shard_map(body, mesh=mesh, in_specs=in_specs, out_specs=out_specs, check_vma=False)
```

```python
import functools

import jax
import jax.numpy as jnp
from jax import lax
from jax.experimental import pallas as pl
from jax.experimental.pallas import tpu as pltpu
from jax.sharding import PartitionSpec as P

STEPS = 3


step_size = 0.15


def extended(block, sides, width):
    for axis, dim in sides:
        count = lax.axis_size(axis)
        forward = [(i, i + 1) for i in range(count - 1)]
        backward = [(target, source) for source, target in forward]
        low = lax.ppermute(
            lax.slice_in_dim(block, block.shape[dim] - width, None, axis=dim), axis, forward
        )
        high = lax.ppermute(lax.slice_in_dim(block, 0, width, axis=dim), axis, backward)
        block = jnp.concatenate([low, block, high], axis=dim)
    return block


def forward_step(state, coeffs):
    padded = extended(state, (("tile", 1),), 1)
    north_rows = padded[:, 2:]
    south_rows = padded[:, :-2]
    east_cells = jnp.roll(state, -1, 2)
    west_cells = jnp.roll(state, 1, 2)
    return (
        state
        + coeffs[0] * (north_rows - state)
        + coeffs[1] * (south_rows - state)
        + coeffs[2] * (east_cells - state)
        + coeffs[3] * (west_cells - state)
    )


def adjoint_step(adjoint, coeffs):
    coef_sum = coeffs[0] + coeffs[1] + coeffs[2] + coeffs[3]
    fluxes = jnp.stack([coeffs[0] * adjoint, coeffs[1] * adjoint])
    padded = extended(fluxes, (("tile", 2),), 1)
    north_flux = padded[0][:, :-2]
    south_flux = padded[1][:, 2:]
    return (
        (1.0 - coef_sum) * adjoint
        + north_flux
        + south_flux
        + jnp.roll(coeffs[2] * adjoint, 1, 2)
        + jnp.roll(coeffs[3] * adjoint, -1, 2)
    )


def window_gradient(total_incr, coefs, obs_weight, innovation):
    state = total_incr
    weighted = []
    for section in range(STEPS):
        state = forward_step(state, coefs)
        weighted.append(obs_weight[section] * (state - innovation[section]))
    adjoint = weighted[STEPS - 1]
    for section in range(STEPS - 2, -1, -1):
        adjoint = adjoint_step(adjoint, coefs) + weighted[section]
    return adjoint_step(adjoint, coefs)


def local(
    level_map,
    loc_lat,
    loc_lon,
    ens_perts,
    ens_control,
    static_control,
    static_scale,
    coefs,
    obs_weight,
    innovation,
):
    tile_count = lax.axis_size("tile")
    my_level = level_map[lax.axis_index("tile")]
    levels = static_control.shape[0]
    level_ids = jnp.arange(levels, dtype=jnp.int32)
    level_onehot = (level_map[:, None] == level_ids[None, :]).astype(jnp.float32)
    control = ens_control
    lat_smoothed = jnp.einsum(
        "ij,bjk->bik", loc_lat, control.astype(jnp.bfloat16), preferred_element_type=jnp.float32
    ).astype(jnp.bfloat16)
    member_field = jnp.einsum(
        "bij,kj->bik", lat_smoothed, loc_lon, preferred_element_type=jnp.float32
    )
    partial_value = jnp.sum(ens_perts.astype(jnp.float32) * member_field, axis=0)
    pieces = partial_value.reshape(tile_count, -1, partial_value.shape[1])
    received = lax.all_to_all(pieces, "tile", split_axis=0, concat_axis=0, tiled=True)
    ens_incr = jnp.einsum("dl,dij->lij", level_onehot, received, precision=lax.Precision.HIGHEST)
    total_incr = static_scale * static_control + ens_incr
    gradient = window_gradient(total_incr, coefs, obs_weight, innovation)
    static_control = static_control - step_size * (static_control + static_scale * gradient)
    gathered = lax.all_gather(gradient, "tile", axis=1, tiled=True)
    grad_field = lax.dynamic_index_in_dim(gathered, my_level, 0, keepdims=False)
    weighted_grad = (ens_perts.astype(jnp.float32) * grad_field[None]).astype(jnp.bfloat16)
    adjoint_lat = jnp.einsum(
        "ji,bjk->bik", loc_lat, weighted_grad, preferred_element_type=jnp.float32
    ).astype(jnp.bfloat16)
    member_grad = jnp.einsum(
        "bij,jk->bik", adjoint_lat, loc_lon, preferred_element_type=jnp.float32
    )
    control = control - step_size * (control + member_grad)
    return (control, static_control)


MESH = pl.DeviceIdType.MESH
SIDE = 4


def kernel(
    n,
    level_hbm,
    lat_hbm,
    lon_hbm,
    perts_hbm,
    control_hbm,
    static_hbm,
    scale_hbm,
    coefs_hbm,
    weight_hbm,
    innov_hbm,
    grad_field,
    static_out,
    lat_out,
    level_map,
    blocks_of,
    lat,
    lon,
    perts,
    control,
    static,
    scale,
    coefs,
    weight,
    innov,
    lat_t,
    field,
    received,
    coef_win,
    keep_win,
    total_win,
    weight_win,
    innov_win,
    weighted,
    early_send,
    early_recv,
    mid_send,
    mid_recv,
    late_send,
    late_recv,
    grad,
    grad_send,
    static_new,
    in_sem,
    out_sem,
    member_send_sem,
    member_recv_sem,
    early_send_sem,
    early_recv_sem,
    mid_send_sem,
    mid_recv_sem,
    late_send_sem,
    late_recv_sem,
    grad_send_sem,
    grad_recv_sem,
):
    me = lax.axis_index("tile")
    levels, rows, cols = static.shape
    nlat = control.shape[0]
    win = rows + 2 * SIDE
    main = slice(SIDE, SIDE + rows)

    def each_level(body, before=None, after=None):
        def two(pair, carry):
            if before is not None:
                before(pair)
            for half in range(2):
                body(pair, half, 2 * pair + half)
            if after is not None:
                after(pair)
            return carry

        lax.fori_loop(0, levels // 2, two, 0)

    loads = {}
    for place, (name, source, target) in enumerate(
        (
            ("control", control_hbm.at[0], control),
            ("lat", lat_hbm, lat),
            ("lon", lon_hbm, lon),
            ("perts", perts_hbm.at[0], perts),
            ("coefs", coefs_hbm, coefs),
            ("static", static_hbm, static),
            ("scale", scale_hbm, scale),
            ("weight", weight_hbm, weight),
            ("innov", innov_hbm, innov),
        )
    ):
        loads[name] = pltpu.make_async_copy(source, target, in_sem.at[place])
        loads[name].start()
    level_load = pltpu.make_async_copy(level_hbm, level_map, out_sem.at[2])
    level_load.start()

    barrier = pltpu.get_barrier_semaphore()
    for d in range(1, n):
        pl.semaphore_signal(
            barrier, inc=1, device_id={"tile": lax.rem(me + d, n)}, device_id_type=MESH
        )

    loads["control"].wait()
    loads["lat"].wait()
    smoothed = jnp.dot(
        lat[...], control[...].astype(jnp.bfloat16), preferred_element_type=jnp.float32
    ).astype(jnp.bfloat16)
    loads["lon"].wait()
    member = lax.dot_general(
        smoothed, lon[...], (((1,), (1,)), ((), ())), preferred_element_type=jnp.float32
    )
    loads["perts"].wait()
    field[...] = perts[...].astype(jnp.float32) * member

    pl.semaphore_wait(barrier, n - 1)

    def piece(tile):
        return pl.ds(pl.multiple_of(tile * rows, 8), rows)

    order = sorted(range(1, n), key=lambda d: abs(2 * d - n))
    member_copies = []
    for d in order:
        peer = lax.rem(me + d, n)
        copy = pltpu.make_async_remote_copy(
            src_ref=field.at[piece(peer)],
            dst_ref=received.at[me],
            send_sem=member_send_sem.at[d],
            recv_sem=member_recv_sem.at[d],
            device_id={"tile": peer},
            device_id_type=MESH,
        )
        copy.start()
        member_copies.append(copy)
    received[me] = field[piece(me), :]

    loads["coefs"].wait()
    loads["static"].wait()
    loads["scale"].wait()

    def early_rows(pair, half, level):
        for k in range(4):
            early_send[0, level, 2 * k : 2 * k + 2, :] = coefs[k, level, rows - 2 : rows, :]
            early_send[1, level, 2 * k : 2 * k + 2, :] = coefs[k, level, 0:2, :]
            coef_win[k, level, main, :] = coefs[k, level]

    each_level(early_rows)

    def exchange(send, recv, send_sem, recv_sem, action, chunk=0, width=None):
        def one(side, target):
            part = (side,) if width is None else (side, pl.ds(chunk * width, width))
            return pltpu.make_async_remote_copy(
                src_ref=send.at[part],
                dst_ref=recv.at[part],
                send_sem=send_sem.at[side, chunk],
                recv_sem=recv_sem.at[side, chunk],
                device_id={"tile": target},
                device_id_type=MESH,
            )

        @pl.when(me < n - 1)
        def _():
            action(0, 1, functools.partial(one, target=me + 1))

        @pl.when(me > 0)
        def _():
            action(1, 0, functools.partial(one, target=me - 1))

    def start(out, back, one):
        one(out).start()

    def wait_recv(out, back, one):
        one(back).wait_recv()

    def wait_send(out, back, one):
        one(out).wait_send()

    early = (early_send, early_recv, early_send_sem, early_recv_sem)
    mid = (mid_send, mid_recv, mid_send_sem, mid_recv_sem)
    late = (late_send, late_recv, late_send_sem, late_recv_sem)
    exchange(*early, start)

    lat_t[...] = lat[...].astype(jnp.float32).T.astype(jnp.bfloat16)
    lat_store = pltpu.make_async_copy(lat_t, lat_out, out_sem.at[1])
    lat_store.start()
    loads["weight"].wait()
    loads["innov"].wait()
    edge = jnp.zeros((SIDE, cols), jnp.float32)

    def widen(pair, half, level):
        for k in range(STEPS):
            for target, source in ((weight_win, weight), (innov_win, innov)):
                target[k, level, 0:SIDE, :] = edge
                target[k, level, main, :] = source[k, level]
                target[k, level, SIDE + rows : win, :] = edge

    each_level(widen)

    level_load.wait()

    def find(level, carry):
        low, high = jnp.int32(n - 1), jnp.int32(0)
        for block in range(n):
            here = level_map[block] == level
            low = jnp.minimum(low, jnp.where(here, block, n - 1))
            high = jnp.maximum(high, jnp.where(here, block, 0))
        blocks_of[0, level] = low
        blocks_of[1, level] = high
        return carry

    lax.fori_loop(0, levels, find, 0)

    exchange(*early, wait_recv)

    @pl.when(me == 0)
    def _():
        early_recv[0] = jnp.zeros(early_recv.shape[1:], jnp.float32)
        mid_recv[0] = jnp.zeros(mid_recv.shape[1:], jnp.float32)
        late_recv[0] = jnp.zeros(late_recv.shape[1:], jnp.float32)

    @pl.when(me == n - 1)
    def _():
        early_recv[1] = jnp.zeros(early_recv.shape[1:], jnp.float32)
        mid_recv[1] = jnp.zeros(mid_recv.shape[1:], jnp.float32)
        late_recv[1] = jnp.zeros(late_recv.shape[1:], jnp.float32)

    def unpack_early(pair, half, level):
        for k in range(4):
            coef_win[k, level, 0 : SIDE - 2, :] = jnp.full(
                (SIDE - 2, cols), 1.0 if k == 0 else 0.0, jnp.float32
            )
            coef_win[k, level, SIDE - 2 : SIDE, :] = early_recv[0, level, 2 * k : 2 * k + 2, :]
            coef_win[k, level, SIDE + rows : SIDE + rows + 2, :] = early_recv[
                1, level, 2 * k : 2 * k + 2, :
            ]
            coef_win[k, level, SIDE + rows + 2 : win, :] = jnp.full(
                (SIDE - 2, cols), 1.0 if k == 1 else 0.0, jnp.float32
            )
        keep_win[level] = 1.0 - (
            coef_win[0, level] + coef_win[1, level] + coef_win[2, level] + coef_win[3, level]
        )

    each_level(unpack_early)

    for copy in member_copies:
        copy.wait_recv()

    def add_up(pair, half, level):
        total = scale[level] * static[level] + (
            received[blocks_of[0, level]] + received[blocks_of[1, level]]
        )
        at = half * SIDE
        mid_send[0, pair, at : at + SIDE, :] = total[rows - SIDE : rows]
        mid_send[1, pair, at : at + SIDE, :] = total[0:SIDE]
        total_win[level, main, :] = total

    each_level(add_up, after=lambda pair: exchange(*mid, start, pair, 1))

    def forward(pair, half, level):
        at = half * SIDE
        total_win[level, 0:SIDE, :] = mid_recv[0, pair, at : at + SIDE, :]
        total_win[level, SIDE + rows : win, :] = mid_recv[1, pair, at : at + SIDE, :]
        state = total_win[level]
        c = [coef_win[k, level] for k in range(4)]
        for k in range(STEPS):
            state = (
                state
                + c[0] * (pltpu.roll(state, win - 1, 0) - state)
                + c[1] * (pltpu.roll(state, 1, 0) - state)
                + c[2] * (pltpu.roll(state, cols - 1, 1) - state)
                + c[3] * (pltpu.roll(state, 1, 1) - state)
            )
            value = weight_win[k, level] * (state - innov_win[k, level])
            weighted[k, level] = value
            at = k * (k + 1) // 2
            low, high = SIDE, SIDE + rows
            near = min(k + 1, 2)
            late_send[0, level, at : at + near, :] = value[high - near : high]
            late_send[1, level, at : at + near, :] = value[low : low + near]
            if k == 2:
                late_send[0, level, at + 2 : at + 3, :] = (c[0] * value)[high - 3 : high - 2]
                late_send[1, level, at + 2 : at + 3, :] = (c[1] * value)[low + 2 : low + 3]

    each_level(
        forward,
        before=lambda pair: exchange(*mid, wait_recv, pair, 1),
        after=lambda pair: exchange(*late, start, pair, 2),
    )

    def backward(pair, half, level):
        for k in range(STEPS):
            at = k * (k + 1) // 2
            low, high = SIDE, SIDE + rows
            near = min(k + 1, 2)
            weighted[k, level, low - near : low, :] = late_recv[0, level, at : at + near, :]
            weighted[k, level, high : high + near, :] = late_recv[1, level, at : at + near, :]
            if k == 2:
                weighted[k, level, low - 3 : low - 2, :] = late_recv[0, level, at + 2 : at + 3, :]
                weighted[k, level, high + 2 : high + 3, :] = late_recv[
                    1, level, at + 2 : at + 3, :
                ]
        adjoint = weighted[STEPS - 1, level]
        c = [coef_win[k, level] for k in range(4)]
        for k in range(STEPS - 2, -2, -1):
            adjoint = (
                keep_win[level] * adjoint
                + pltpu.roll(c[0] * adjoint, 1, 0)
                + pltpu.roll(c[1] * adjoint, win - 1, 0)
                + pltpu.roll(c[2] * adjoint, 1, 1)
                + pltpu.roll(c[3] * adjoint, cols - 1, 1)
            )
            if k >= 0:
                adjoint = adjoint + weighted[k, level]
        grad[level] = adjoint[SIDE : SIDE + rows]

    each_level(backward, before=lambda pair: exchange(*late, wait_recv, pair, 2))

    grad_copies = []
    for d in order:
        peer = lax.rem(me + d, n)
        grad_send[d] = grad[level_map[peer]]
        copy = pltpu.make_async_remote_copy(
            src_ref=grad_send.at[d],
            dst_ref=grad_field.at[me],
            send_sem=grad_send_sem.at[d],
            recv_sem=grad_recv_sem.at[d],
            device_id={"tile": peer},
            device_id_type=MESH,
        )
        copy.start()
        grad_copies.append(copy)
    grad_send[0] = grad[level_map[me]]
    own_store = pltpu.make_async_copy(grad_send.at[0], grad_field.at[me], out_sem.at[3])
    own_store.start()

    static_new[...] = static[...] - step_size * (static[...] + scale[...] * grad[...])
    static_store = pltpu.make_async_copy(static_new, static_out, out_sem.at[0])
    static_store.start()

    for copy in member_copies:
        copy.wait_send()
    exchange(*early, wait_send)

    def sent(pair):
        exchange(*mid, wait_send, pair, 1)
        exchange(*late, wait_send, pair, 2)

    each_level(lambda *_: None, before=sent)
    for copy in grad_copies:
        copy.wait_recv()
    for copy in grad_copies:
        copy.wait_send()
    lat_store.wait()
    own_store.wait()
    static_store.wait()


def finish_kernel(
    grad_hbm,
    lat_hbm,
    lon_hbm,
    perts_hbm,
    control_hbm,
    static_hbm,
    ens_out,
    static_out,
    gradient,
    lat_t,
    lon,
    perts,
    control,
    ens_new,
    in_sem,
    out_sem,
):
    loads = []
    for place, (source, target) in enumerate(
        (
            (grad_hbm, gradient),
            (perts_hbm.at[0], perts),
            (lat_hbm, lat_t),
            (lon_hbm, lon),
            (control_hbm.at[0], control),
        )
    ):
        loads.append(pltpu.make_async_copy(source, target, in_sem.at[place]))
        loads[-1].start()
    static_store = pltpu.make_async_copy(static_hbm, static_out, out_sem.at[2])
    static_store.start()
    for load in loads:
        load.wait()
    nlat, cols = control.shape
    grad_field = gradient[...].reshape(nlat, cols)
    weighted_grad = (perts[...].astype(jnp.float32) * grad_field).astype(jnp.bfloat16)
    stores = []
    for part in range(2):
        here = slice(part * nlat // 2, (part + 1) * nlat // 2)
        adjoint_lat = jnp.dot(
            lat_t[here, :], weighted_grad, preferred_element_type=jnp.float32
        ).astype(jnp.bfloat16)
        member_grad = jnp.dot(adjoint_lat, lon[...], preferred_element_type=jnp.float32)
        ens_new[here, :] = control[here, :] - step_size * (control[here, :] + member_grad)
        stores.append(
            pltpu.make_async_copy(ens_new.at[here], ens_out.at[0, here], out_sem.at[part])
        )
        stores[-1].start()
    for store in stores:
        store.wait()
    static_store.wait()


def fused(n, *args):
    level_map, loc_lat, loc_lon, ens_perts, ens_control, static_control = args[:6]
    nlat, cols = ens_control.shape[1:]
    levels, rows, _ = static_control.shape
    win = rows + 2 * SIDE
    f32, bf16 = jnp.float32, jnp.bfloat16
    anywhere = pl.BlockSpec(memory_space=pl.ANY)
    dma = pltpu.SemaphoreType.DMA
    fields = (levels, rows, cols)
    windows = (levels, win, cols)
    grad_field, static_new, lat_t = pl.pallas_call(
        functools.partial(kernel, n),
        out_shape=(
            jax.ShapeDtypeStruct((n, rows, cols), f32),
            jax.ShapeDtypeStruct(static_control.shape, f32),
            jax.ShapeDtypeStruct(loc_lat.shape, bf16),
        ),
        in_specs=[pl.BlockSpec(memory_space=pltpu.HBM)] * 10,
        out_specs=(anywhere, anywhere, anywhere),
        scratch_shapes=[
            pltpu.SMEM(level_map.shape, jnp.int32),
            pltpu.SMEM((2, levels), jnp.int32),
            pltpu.VMEM(loc_lat.shape, bf16),
            pltpu.VMEM(loc_lon.shape, bf16),
            pltpu.VMEM((nlat, cols), bf16),
            pltpu.VMEM((nlat, cols), f32),
            pltpu.VMEM(fields, f32),
            pltpu.VMEM(fields, f32),
            pltpu.VMEM((4,) + fields, f32),
            pltpu.VMEM((STEPS,) + fields, f32),
            pltpu.VMEM((STEPS,) + fields, f32),
            pltpu.VMEM(loc_lat.shape, bf16),
            pltpu.VMEM((nlat, cols), f32),
            pltpu.VMEM((n, rows, cols), f32),
            pltpu.VMEM((4,) + windows, f32),
            pltpu.VMEM(windows, f32),
            pltpu.VMEM(windows, f32),
            pltpu.VMEM((STEPS,) + windows, f32),
            pltpu.VMEM((STEPS,) + windows, f32),
            pltpu.VMEM((STEPS,) + windows, f32),
            pltpu.VMEM((2, levels, 8, cols), f32),
            pltpu.VMEM((2, levels, 8, cols), f32),
            pltpu.VMEM((2, levels // 2, 8, cols), f32),
            pltpu.VMEM((2, levels // 2, 8, cols), f32),
            pltpu.VMEM((2, levels, 8, cols), f32),
            pltpu.VMEM((2, levels, 8, cols), f32),
            pltpu.VMEM(fields, f32),
            pltpu.VMEM((n, rows, cols), f32),
            pltpu.VMEM(fields, f32),
            dma((9,)),
            dma((4,)),
            dma((n,)),
            dma((n,)),
            dma((2, 1)),
            dma((2, 1)),
            dma((2, levels // 2)),
            dma((2, levels // 2)),
            dma((2, levels // 2)),
            dma((2, levels // 2)),
            dma((n,)),
            dma((n,)),
        ],
        compiler_params=pltpu.CompilerParams(
            collective_id=0, has_side_effects=True
        ),
    )(*args)
    return pl.pallas_call(
        finish_kernel,
        out_shape=(
            jax.ShapeDtypeStruct(ens_control.shape, f32),
            jax.ShapeDtypeStruct(static_control.shape, f32),
        ),
        in_specs=[anywhere] * 6,
        out_specs=(anywhere, anywhere),
        scratch_shapes=[
            pltpu.VMEM((n, rows, cols), f32),
            pltpu.VMEM(loc_lat.shape, bf16),
            pltpu.VMEM(loc_lon.shape, bf16),
            pltpu.VMEM((nlat, cols), bf16),
            pltpu.VMEM((nlat, cols), f32),
            pltpu.VMEM((nlat, cols), f32),
            dma((5,)),
            dma((3,)),
        ],
    )(grad_field, lat_t, loc_lon, ens_perts, ens_control, static_new)


def device_program(n, *args):
    ens_control, static_control = args[4:6]
    levels, rows, cols = static_control.shape
    fits = (
        ens_control.shape[0] == 1
        and n == 2 * levels
        and rows % 8 == 0
        and rows * n == ens_control.shape[1]
        and cols % 128 == 0
        and levels % 2 == 0
        and STEPS == 3
    )
    return fused(n, *args) if fits else local(*args)


def solution(mesh):
    in_specs = (
        P(),
        P(),
        P(),
        P(("groups", "tile"), None, None),
        P(("groups", "tile"), None, None),
        P("groups", "tile", None),
        P("groups", "tile", None),
        P(None, "groups", "tile", None),
        P(None, "groups", "tile", None),
        P(None, "groups", "tile", None),
    )
    out_specs = (P(("groups", "tile"), None, None), P("groups", "tile", None))
    body = functools.partial(device_program, mesh.shape["tile"])
    return jax.shard_map(body, mesh=mesh, in_specs=in_specs, out_specs=out_specs, check_vma=False)
```

```python
import functools

import jax
import jax.numpy as jnp
from jax import lax
from jax.experimental import pallas as pl
from jax.experimental.pallas import tpu as pltpu
from jax.sharding import PartitionSpec as P

STEPS = 3


step_size = 0.15


def extended(block, sides, width):
    for axis, dim in sides:
        count = lax.axis_size(axis)
        forward = [(i, i + 1) for i in range(count - 1)]
        backward = [(target, source) for source, target in forward]
        low = lax.ppermute(
            lax.slice_in_dim(block, block.shape[dim] - width, None, axis=dim), axis, forward
        )
        high = lax.ppermute(lax.slice_in_dim(block, 0, width, axis=dim), axis, backward)
        block = jnp.concatenate([low, block, high], axis=dim)
    return block


def forward_step(state, coeffs):
    padded = extended(state, (("tile", 1),), 1)
    north_rows = padded[:, 2:]
    south_rows = padded[:, :-2]
    east_cells = jnp.roll(state, -1, 2)
    west_cells = jnp.roll(state, 1, 2)
    return (
        state
        + coeffs[0] * (north_rows - state)
        + coeffs[1] * (south_rows - state)
        + coeffs[2] * (east_cells - state)
        + coeffs[3] * (west_cells - state)
    )


def adjoint_step(adjoint, coeffs):
    coef_sum = coeffs[0] + coeffs[1] + coeffs[2] + coeffs[3]
    fluxes = jnp.stack([coeffs[0] * adjoint, coeffs[1] * adjoint])
    padded = extended(fluxes, (("tile", 2),), 1)
    north_flux = padded[0][:, :-2]
    south_flux = padded[1][:, 2:]
    return (
        (1.0 - coef_sum) * adjoint
        + north_flux
        + south_flux
        + jnp.roll(coeffs[2] * adjoint, 1, 2)
        + jnp.roll(coeffs[3] * adjoint, -1, 2)
    )


def window_gradient(total_incr, coefs, obs_weight, innovation):
    state = total_incr
    weighted = []
    for section in range(STEPS):
        state = forward_step(state, coefs)
        weighted.append(obs_weight[section] * (state - innovation[section]))
    adjoint = weighted[STEPS - 1]
    for section in range(STEPS - 2, -1, -1):
        adjoint = adjoint_step(adjoint, coefs) + weighted[section]
    return adjoint_step(adjoint, coefs)


def local(
    level_map,
    loc_lat,
    loc_lon,
    ens_perts,
    ens_control,
    static_control,
    static_scale,
    coefs,
    obs_weight,
    innovation,
):
    tile_count = lax.axis_size("tile")
    my_level = level_map[lax.axis_index("tile")]
    levels = static_control.shape[0]
    level_ids = jnp.arange(levels, dtype=jnp.int32)
    level_onehot = (level_map[:, None] == level_ids[None, :]).astype(jnp.float32)
    control = ens_control
    lat_smoothed = jnp.einsum(
        "ij,bjk->bik", loc_lat, control.astype(jnp.bfloat16), preferred_element_type=jnp.float32
    ).astype(jnp.bfloat16)
    member_field = jnp.einsum(
        "bij,kj->bik", lat_smoothed, loc_lon, preferred_element_type=jnp.float32
    )
    partial_value = jnp.sum(ens_perts.astype(jnp.float32) * member_field, axis=0)
    pieces = partial_value.reshape(tile_count, -1, partial_value.shape[1])
    received = lax.all_to_all(pieces, "tile", split_axis=0, concat_axis=0, tiled=True)
    ens_incr = jnp.einsum("dl,dij->lij", level_onehot, received, precision=lax.Precision.HIGHEST)
    total_incr = static_scale * static_control + ens_incr
    gradient = window_gradient(total_incr, coefs, obs_weight, innovation)
    static_control = static_control - step_size * (static_control + static_scale * gradient)
    gathered = lax.all_gather(gradient, "tile", axis=1, tiled=True)
    grad_field = lax.dynamic_index_in_dim(gathered, my_level, 0, keepdims=False)
    weighted_grad = (ens_perts.astype(jnp.float32) * grad_field[None]).astype(jnp.bfloat16)
    adjoint_lat = jnp.einsum(
        "ji,bjk->bik", loc_lat, weighted_grad, preferred_element_type=jnp.float32
    ).astype(jnp.bfloat16)
    member_grad = jnp.einsum(
        "bij,jk->bik", adjoint_lat, loc_lon, preferred_element_type=jnp.float32
    )
    control = control - step_size * (control + member_grad)
    return (control, static_control)


MESH = pl.DeviceIdType.MESH
SIDE = 4


def kernel(
    n,
    level_hbm,
    lat_hbm,
    lon_hbm,
    perts_hbm,
    control_hbm,
    static_hbm,
    scale_hbm,
    coefs_hbm,
    weight_hbm,
    innov_hbm,
    grad_field,
    static_out,
    lat_out,
    level_map,
    blocks_of,
    lat,
    lon,
    perts,
    control,
    static,
    scale,
    coefs,
    weight,
    innov,
    lat_t,
    field,
    received,
    coef_win,
    keep_win,
    total_win,
    weight_win,
    innov_win,
    weighted,
    early_send,
    early_recv,
    late_send,
    late_recv,
    grad,
    grad_send,
    static_new,
    in_sem,
    out_sem,
    member_send_sem,
    member_recv_sem,
    early_send_sem,
    early_recv_sem,
    late_send_sem,
    late_recv_sem,
    grad_send_sem,
    grad_recv_sem,
):
    me = lax.axis_index("tile")
    levels, rows, cols = static.shape
    nlat = control.shape[0]
    win = rows + 2 * SIDE
    main = slice(SIDE, SIDE + rows)

    def each_level(body, before=None, after=None):
        def two(pair, carry):
            if before is not None:
                before(pair)
            for half in range(2):
                body(pair, half, 2 * pair + half)
            if after is not None:
                after(pair)
            return carry

        lax.fori_loop(0, levels // 2, two, 0)

    loads = {}
    for place, (name, source, target) in enumerate(
        (
            ("control", control_hbm.at[0], control),
            ("lat", lat_hbm, lat),
            ("lon", lon_hbm, lon),
            ("perts", perts_hbm.at[0], perts),
            ("coefs", coefs_hbm, coefs),
            ("static", static_hbm, static),
            ("scale", scale_hbm, scale),
            ("weight", weight_hbm, weight),
            ("innov", innov_hbm, innov),
        )
    ):
        loads[name] = pltpu.make_async_copy(source, target, in_sem.at[place])
        loads[name].start()
    level_load = pltpu.make_async_copy(level_hbm, level_map, out_sem.at[2])
    level_load.start()

    barrier = pltpu.get_barrier_semaphore()
    for d in range(1, n):
        pl.semaphore_signal(
            barrier, inc=1, device_id={"tile": lax.rem(me + d, n)}, device_id_type=MESH
        )

    loads["control"].wait()
    loads["lat"].wait()
    smoothed = jnp.dot(
        lat[...], control[...].astype(jnp.bfloat16), preferred_element_type=jnp.float32
    ).astype(jnp.bfloat16)
    loads["lon"].wait()
    member = lax.dot_general(
        smoothed, lon[...], (((1,), (1,)), ((), ())), preferred_element_type=jnp.float32
    )
    loads["perts"].wait()
    field[0:SIDE, :] = jnp.zeros((SIDE, cols), jnp.float32)
    field[SIDE + nlat : 2 * SIDE + nlat, :] = jnp.zeros((SIDE, cols), jnp.float32)
    field[SIDE : SIDE + nlat, :] = perts[...].astype(jnp.float32) * member

    pl.semaphore_wait(barrier, n - 1)

    def window(tile):
        return pl.ds(pl.multiple_of(tile * rows, 8), win)

    order = sorted(range(1, n), key=lambda d: abs(2 * d - n))
    member_copies = []
    for d in order:
        peer = lax.rem(me + d, n)
        copy = pltpu.make_async_remote_copy(
            src_ref=field.at[window(peer)],
            dst_ref=received.at[me],
            send_sem=member_send_sem.at[d],
            recv_sem=member_recv_sem.at[d],
            device_id={"tile": peer},
            device_id_type=MESH,
        )
        copy.start()
        member_copies.append(copy)
    received[me] = field[window(me), :]

    loads["coefs"].wait()
    loads["static"].wait()
    loads["scale"].wait()

    def early_rows(pair, half, level):
        for k in range(4):
            early_send[0, level, 2 * k : 2 * k + 2, :] = coefs[k, level, rows - 2 : rows, :]
            early_send[1, level, 2 * k : 2 * k + 2, :] = coefs[k, level, 0:2, :]
            coef_win[k, level, main, :] = coefs[k, level]
        value = scale[level] * static[level]
        at = half * SIDE
        early_send[0, levels + pair, at : at + SIDE, :] = value[rows - SIDE : rows]
        early_send[1, levels + pair, at : at + SIDE, :] = value[0:SIDE]
        total_win[level, main, :] = value

    each_level(early_rows)

    def exchange(send, recv, send_sem, recv_sem, action, chunk=0, width=None):
        def one(side, target):
            part = (side,) if width is None else (side, pl.ds(chunk * width, width))
            return pltpu.make_async_remote_copy(
                src_ref=send.at[part],
                dst_ref=recv.at[part],
                send_sem=send_sem.at[side, chunk],
                recv_sem=recv_sem.at[side, chunk],
                device_id={"tile": target},
                device_id_type=MESH,
            )

        @pl.when(me < n - 1)
        def _():
            action(0, 1, functools.partial(one, target=me + 1))

        @pl.when(me > 0)
        def _():
            action(1, 0, functools.partial(one, target=me - 1))

    def start(out, back, one):
        one(out).start()

    def wait_recv(out, back, one):
        one(back).wait_recv()

    def wait_send(out, back, one):
        one(out).wait_send()

    early = (early_send, early_recv, early_send_sem, early_recv_sem)
    late = (late_send, late_recv, late_send_sem, late_recv_sem)
    exchange(*early, start)

    lat_t[...] = lat[...].astype(jnp.float32).T.astype(jnp.bfloat16)
    lat_store = pltpu.make_async_copy(lat_t, lat_out, out_sem.at[1])
    lat_store.start()
    loads["weight"].wait()
    loads["innov"].wait()
    edge = jnp.zeros((SIDE, cols), jnp.float32)

    def widen(pair, half, level):
        for k in range(STEPS):
            for target, source in ((weight_win, weight), (innov_win, innov)):
                target[k, level, 0:SIDE, :] = edge
                target[k, level, main, :] = source[k, level]
                target[k, level, SIDE + rows : win, :] = edge

    each_level(widen)

    level_load.wait()

    def find(level, carry):
        low, high = jnp.int32(n - 1), jnp.int32(0)
        for block in range(n):
            here = level_map[block] == level
            low = jnp.minimum(low, jnp.where(here, block, n - 1))
            high = jnp.maximum(high, jnp.where(here, block, 0))
        blocks_of[0, level] = low
        blocks_of[1, level] = high
        return carry

    lax.fori_loop(0, levels, find, 0)

    exchange(*early, wait_recv)

    @pl.when(me == 0)
    def _():
        early_recv[0] = jnp.zeros(early_recv.shape[1:], jnp.float32)
        late_recv[0] = jnp.zeros(late_recv.shape[1:], jnp.float32)

    @pl.when(me == n - 1)
    def _():
        early_recv[1] = jnp.zeros(early_recv.shape[1:], jnp.float32)
        late_recv[1] = jnp.zeros(late_recv.shape[1:], jnp.float32)

    def unpack_early(pair, half, level):
        for k in range(4):
            coef_win[k, level, 0 : SIDE - 2, :] = jnp.full(
                (SIDE - 2, cols), 1.0 if k == 0 else 0.0, jnp.float32
            )
            coef_win[k, level, SIDE - 2 : SIDE, :] = early_recv[0, level, 2 * k : 2 * k + 2, :]
            coef_win[k, level, SIDE + rows : SIDE + rows + 2, :] = early_recv[
                1, level, 2 * k : 2 * k + 2, :
            ]
            coef_win[k, level, SIDE + rows + 2 : win, :] = jnp.full(
                (SIDE - 2, cols), 1.0 if k == 1 else 0.0, jnp.float32
            )
        at = half * SIDE
        total_win[level, 0:SIDE, :] = early_recv[0, levels + pair, at : at + SIDE, :]
        total_win[level, SIDE + rows : win, :] = early_recv[1, levels + pair, at : at + SIDE, :]
        keep_win[level] = 1.0 - (
            coef_win[0, level] + coef_win[1, level] + coef_win[2, level] + coef_win[3, level]
        )

    each_level(unpack_early)

    for copy in member_copies:
        copy.wait_recv()

    def forward(pair, half, level):
        state = total_win[level] + (received[blocks_of[0, level]] + received[blocks_of[1, level]])
        c = [coef_win[k, level] for k in range(4)]
        keep = keep_win[level]
        for k in range(STEPS):
            state = (
                keep * state
                + c[0] * pltpu.roll(state, win - 1, 0)
                + c[1] * pltpu.roll(state, 1, 0)
                + c[2] * pltpu.roll(state, cols - 1, 1)
                + c[3] * pltpu.roll(state, 1, 1)
            )
            value = weight_win[k, level] * (state - innov_win[k, level])
            weighted[k, level] = value
            at = k * (k + 1) // 2
            low, high = SIDE, SIDE + rows
            near = min(k + 1, 2)
            late_send[0, level, at : at + near, :] = value[high - near : high]
            late_send[1, level, at : at + near, :] = value[low : low + near]
            if k == 2:
                late_send[0, level, at + 2 : at + 3, :] = (c[0] * value)[high - 3 : high - 2]
                late_send[1, level, at + 2 : at + 3, :] = (c[1] * value)[low + 2 : low + 3]

    each_level(
        forward,
        after=lambda pair: exchange(*late, start, pair, 2),
    )

    def backward(pair, half, level):
        for k in range(STEPS):
            at = k * (k + 1) // 2
            low, high = SIDE, SIDE + rows
            near = min(k + 1, 2)
            weighted[k, level, low - near : low, :] = late_recv[0, level, at : at + near, :]
            weighted[k, level, high : high + near, :] = late_recv[1, level, at : at + near, :]
            if k == 2:
                weighted[k, level, low - 3 : low - 2, :] = late_recv[0, level, at + 2 : at + 3, :]
                weighted[k, level, high + 2 : high + 3, :] = late_recv[
                    1, level, at + 2 : at + 3, :
                ]
        adjoint = weighted[STEPS - 1, level]
        c = [coef_win[k, level] for k in range(4)]
        for k in range(STEPS - 2, -2, -1):
            adjoint = (
                keep_win[level] * adjoint
                + pltpu.roll(c[0] * adjoint, 1, 0)
                + pltpu.roll(c[1] * adjoint, win - 1, 0)
                + pltpu.roll(c[2] * adjoint, 1, 1)
                + pltpu.roll(c[3] * adjoint, cols - 1, 1)
            )
            if k >= 0:
                adjoint = adjoint + weighted[k, level]
        grad[level] = adjoint[SIDE : SIDE + rows]

    each_level(backward, before=lambda pair: exchange(*late, wait_recv, pair, 2))

    grad_copies = []
    for d in order:
        peer = lax.rem(me + d, n)
        grad_send[d] = grad[level_map[peer]]
        copy = pltpu.make_async_remote_copy(
            src_ref=grad_send.at[d],
            dst_ref=grad_field.at[me],
            send_sem=grad_send_sem.at[d],
            recv_sem=grad_recv_sem.at[d],
            device_id={"tile": peer},
            device_id_type=MESH,
        )
        copy.start()
        grad_copies.append(copy)
    grad_send[0] = grad[level_map[me]]
    own_store = pltpu.make_async_copy(grad_send.at[0], grad_field.at[me], out_sem.at[3])
    own_store.start()

    static_new[...] = static[...] - step_size * (static[...] + scale[...] * grad[...])
    static_store = pltpu.make_async_copy(static_new, static_out, out_sem.at[0])
    static_store.start()

    for copy in member_copies:
        copy.wait_send()
    exchange(*early, wait_send)

    def sent(pair):
        exchange(*late, wait_send, pair, 2)

    each_level(lambda *_: None, before=sent)
    for copy in grad_copies:
        copy.wait_recv()
    for copy in grad_copies:
        copy.wait_send()
    lat_store.wait()
    own_store.wait()
    static_store.wait()


def finish_kernel(
    grad_hbm,
    lat_hbm,
    lon_hbm,
    perts_hbm,
    control_hbm,
    static_hbm,
    ens_out,
    static_out,
    gradient,
    lat_t,
    lon,
    perts,
    control,
    ens_new,
    static_new,
    in_sem,
    out_sem,
):
    loads = []
    for place, (source, target) in enumerate(
        (
            (grad_hbm, gradient),
            (perts_hbm.at[0], perts),
            (lat_hbm, lat_t),
            (lon_hbm, lon),
            (control_hbm.at[0], control),
            (static_hbm, static_new),
        )
    ):
        loads.append(pltpu.make_async_copy(source, target, in_sem.at[place]))
        loads[-1].start()
    loads[0].wait()
    loads[1].wait()
    nlat, cols = control.shape
    grad_field = gradient[...].reshape(nlat, cols)
    weighted_grad = (perts[...].astype(jnp.float32) * grad_field).astype(jnp.bfloat16)
    for load in loads[2:]:
        load.wait()
    stores = [pltpu.make_async_copy(static_new, static_out, out_sem.at[2])]
    stores[0].start()
    for part in range(2):
        here = slice(part * nlat // 2, (part + 1) * nlat // 2)
        adjoint_lat = jnp.dot(
            lat_t[here, :], weighted_grad, preferred_element_type=jnp.float32
        ).astype(jnp.bfloat16)
        member_grad = jnp.dot(adjoint_lat, lon[...], preferred_element_type=jnp.float32)
        ens_new[here, :] = control[here, :] - step_size * (control[here, :] + member_grad)
        stores.append(
            pltpu.make_async_copy(ens_new.at[here], ens_out.at[0, here], out_sem.at[part])
        )
        stores[-1].start()
    for store in stores:
        store.wait()


def fused(n, *args):
    level_map, loc_lat, loc_lon, ens_perts, ens_control, static_control = args[:6]
    nlat, cols = ens_control.shape[1:]
    levels, rows, _ = static_control.shape
    win = rows + 2 * SIDE
    f32, bf16 = jnp.float32, jnp.bfloat16
    anywhere = pl.BlockSpec(memory_space=pl.ANY)
    dma = pltpu.SemaphoreType.DMA
    fields = (levels, rows, cols)
    windows = (levels, win, cols)
    grad_field, static_new, lat_t = pl.pallas_call(
        functools.partial(kernel, n),
        out_shape=(
            jax.ShapeDtypeStruct((n, rows, cols), f32),
            jax.ShapeDtypeStruct(static_control.shape, f32),
            jax.ShapeDtypeStruct(loc_lat.shape, bf16),
        ),
        in_specs=[pl.BlockSpec(memory_space=pltpu.HBM)] * 10,
        out_specs=(anywhere, anywhere, anywhere),
        scratch_shapes=[
            pltpu.SMEM(level_map.shape, jnp.int32),
            pltpu.SMEM((2, levels), jnp.int32),
            pltpu.VMEM(loc_lat.shape, bf16),
            pltpu.VMEM(loc_lon.shape, bf16),
            pltpu.VMEM((nlat, cols), bf16),
            pltpu.VMEM((nlat, cols), f32),
            pltpu.VMEM(fields, f32),
            pltpu.VMEM(fields, f32),
            pltpu.VMEM((4,) + fields, f32),
            pltpu.VMEM((STEPS,) + fields, f32),
            pltpu.VMEM((STEPS,) + fields, f32),
            pltpu.VMEM(loc_lat.shape, bf16),
            pltpu.VMEM((nlat + 2 * SIDE, cols), f32),
            pltpu.VMEM((n, win, cols), f32),
            pltpu.VMEM((4,) + windows, f32),
            pltpu.VMEM(windows, f32),
            pltpu.VMEM(windows, f32),
            pltpu.VMEM((STEPS,) + windows, f32),
            pltpu.VMEM((STEPS,) + windows, f32),
            pltpu.VMEM((STEPS,) + windows, f32),
            pltpu.VMEM((2, levels + levels // 2, 8, cols), f32),
            pltpu.VMEM((2, levels + levels // 2, 8, cols), f32),
            pltpu.VMEM((2, levels, 8, cols), f32),
            pltpu.VMEM((2, levels, 8, cols), f32),
            pltpu.VMEM(fields, f32),
            pltpu.VMEM((n, rows, cols), f32),
            pltpu.VMEM(fields, f32),
            dma((9,)),
            dma((4,)),
            dma((n,)),
            dma((n,)),
            dma((2, 1)),
            dma((2, 1)),
            dma((2, levels // 2)),
            dma((2, levels // 2)),
            dma((n,)),
            dma((n,)),
        ],
        compiler_params=pltpu.CompilerParams(
            collective_id=0, has_side_effects=True
        ),
    )(*args)
    return pl.pallas_call(
        finish_kernel,
        out_shape=(
            jax.ShapeDtypeStruct(ens_control.shape, f32),
            jax.ShapeDtypeStruct(static_control.shape, f32),
        ),
        in_specs=[anywhere] * 6,
        out_specs=(anywhere, anywhere),
        scratch_shapes=[
            pltpu.VMEM((n, rows, cols), f32),
            pltpu.VMEM(loc_lat.shape, bf16),
            pltpu.VMEM(loc_lon.shape, bf16),
            pltpu.VMEM((nlat, cols), bf16),
            pltpu.VMEM((nlat, cols), f32),
            pltpu.VMEM((nlat, cols), f32),
            pltpu.VMEM(fields, f32),
            dma((6,)),
            dma((3,)),
        ],
    )(grad_field, lat_t, loc_lon, ens_perts, ens_control, static_new)


def device_program(n, *args):
    ens_control, static_control = args[4:6]
    levels, rows, cols = static_control.shape
    fits = (
        ens_control.shape[0] == 1
        and n == 2 * levels
        and rows % 8 == 0
        and rows * n == ens_control.shape[1]
        and cols % 128 == 0
        and levels % 2 == 0
        and STEPS == 3
    )
    return fused(n, *args) if fits else local(*args)


def solution(mesh):
    in_specs = (
        P(),
        P(),
        P(),
        P(("groups", "tile"), None, None),
        P(("groups", "tile"), None, None),
        P("groups", "tile", None),
        P("groups", "tile", None),
        P(None, "groups", "tile", None),
        P(None, "groups", "tile", None),
        P(None, "groups", "tile", None),
    )
    out_specs = (P(("groups", "tile"), None, None), P("groups", "tile", None))
    body = functools.partial(device_program, mesh.shape["tile"])
    return jax.shard_map(body, mesh=mesh, in_specs=in_specs, out_specs=out_specs, check_vma=False)
```

```python
import functools

import jax
import jax.numpy as jnp
from jax import lax
from jax.experimental import pallas as pl
from jax.experimental.pallas import tpu as pltpu
from jax.sharding import PartitionSpec as P

STEPS = 3


step_size = 0.15


def extended(block, sides, width):
    for axis, dim in sides:
        count = lax.axis_size(axis)
        forward = [(i, i + 1) for i in range(count - 1)]
        backward = [(target, source) for source, target in forward]
        low = lax.ppermute(
            lax.slice_in_dim(block, block.shape[dim] - width, None, axis=dim), axis, forward
        )
        high = lax.ppermute(lax.slice_in_dim(block, 0, width, axis=dim), axis, backward)
        block = jnp.concatenate([low, block, high], axis=dim)
    return block


def forward_step(state, coeffs):
    padded = extended(state, (("tile", 1),), 1)
    north_rows = padded[:, 2:]
    south_rows = padded[:, :-2]
    east_cells = jnp.roll(state, -1, 2)
    west_cells = jnp.roll(state, 1, 2)
    return (
        state
        + coeffs[0] * (north_rows - state)
        + coeffs[1] * (south_rows - state)
        + coeffs[2] * (east_cells - state)
        + coeffs[3] * (west_cells - state)
    )


def adjoint_step(adjoint, coeffs):
    coef_sum = coeffs[0] + coeffs[1] + coeffs[2] + coeffs[3]
    fluxes = jnp.stack([coeffs[0] * adjoint, coeffs[1] * adjoint])
    padded = extended(fluxes, (("tile", 2),), 1)
    north_flux = padded[0][:, :-2]
    south_flux = padded[1][:, 2:]
    return (
        (1.0 - coef_sum) * adjoint
        + north_flux
        + south_flux
        + jnp.roll(coeffs[2] * adjoint, 1, 2)
        + jnp.roll(coeffs[3] * adjoint, -1, 2)
    )


def window_gradient(total_incr, coefs, obs_weight, innovation):
    state = total_incr
    weighted = []
    for section in range(STEPS):
        state = forward_step(state, coefs)
        weighted.append(obs_weight[section] * (state - innovation[section]))
    adjoint = weighted[STEPS - 1]
    for section in range(STEPS - 2, -1, -1):
        adjoint = adjoint_step(adjoint, coefs) + weighted[section]
    return adjoint_step(adjoint, coefs)


def local(
    level_map,
    loc_lat,
    loc_lon,
    ens_perts,
    ens_control,
    static_control,
    static_scale,
    coefs,
    obs_weight,
    innovation,
):
    tile_count = lax.axis_size("tile")
    my_level = level_map[lax.axis_index("tile")]
    levels = static_control.shape[0]
    level_ids = jnp.arange(levels, dtype=jnp.int32)
    level_onehot = (level_map[:, None] == level_ids[None, :]).astype(jnp.float32)
    control = ens_control
    lat_smoothed = jnp.einsum(
        "ij,bjk->bik", loc_lat, control.astype(jnp.bfloat16), preferred_element_type=jnp.float32
    ).astype(jnp.bfloat16)
    member_field = jnp.einsum(
        "bij,kj->bik", lat_smoothed, loc_lon, preferred_element_type=jnp.float32
    )
    partial_value = jnp.sum(ens_perts.astype(jnp.float32) * member_field, axis=0)
    pieces = partial_value.reshape(tile_count, -1, partial_value.shape[1])
    received = lax.all_to_all(pieces, "tile", split_axis=0, concat_axis=0, tiled=True)
    ens_incr = jnp.einsum("dl,dij->lij", level_onehot, received, precision=lax.Precision.HIGHEST)
    total_incr = static_scale * static_control + ens_incr
    gradient = window_gradient(total_incr, coefs, obs_weight, innovation)
    static_control = static_control - step_size * (static_control + static_scale * gradient)
    gathered = lax.all_gather(gradient, "tile", axis=1, tiled=True)
    grad_field = lax.dynamic_index_in_dim(gathered, my_level, 0, keepdims=False)
    weighted_grad = (ens_perts.astype(jnp.float32) * grad_field[None]).astype(jnp.bfloat16)
    adjoint_lat = jnp.einsum(
        "ji,bjk->bik", loc_lat, weighted_grad, preferred_element_type=jnp.float32
    ).astype(jnp.bfloat16)
    member_grad = jnp.einsum(
        "bij,jk->bik", adjoint_lat, loc_lon, preferred_element_type=jnp.float32
    )
    control = control - step_size * (control + member_grad)
    return (control, static_control)


MESH = pl.DeviceIdType.MESH
SIDE = 4


def kernel(
    n,
    level_hbm,
    lat_hbm,
    lon_hbm,
    perts_hbm,
    control_hbm,
    static_hbm,
    scale_hbm,
    coefs_hbm,
    weight_hbm,
    innov_hbm,
    grad_field,
    static_out,
    lat_out,
    level_map,
    blocks_of,
    lat,
    lon,
    perts,
    control,
    static,
    scale,
    coefs,
    weight,
    innov,
    lat_t,
    field,
    received,
    coef_win,
    keep_win,
    total_win,
    weight_win,
    innov_win,
    weighted,
    early_send,
    early_recv,
    late_send,
    late_recv,
    grad,
    grad_send,
    static_new,
    in_sem,
    out_sem,
    member_send_sem,
    member_recv_sem,
    early_send_sem,
    early_recv_sem,
    late_send_sem,
    late_recv_sem,
    grad_send_sem,
    grad_recv_sem,
):
    me = lax.axis_index("tile")
    levels, rows, cols = static.shape
    nlat = control.shape[0]
    win = rows + 2 * SIDE
    main = slice(SIDE, SIDE + rows)

    def each_level(body, before=None, after=None):
        def two(pair, carry):
            if before is not None:
                before(pair)
            for half in range(2):
                body(pair, half, 2 * pair + half)
            if after is not None:
                after(pair)
            return carry

        lax.fori_loop(0, levels // 2, two, 0)

    loads = {}
    for place, (name, source, target) in enumerate(
        (
            ("control", control_hbm.at[0], control),
            ("lat", lat_hbm, lat),
            ("lon", lon_hbm, lon),
            ("perts", perts_hbm.at[0], perts),
            ("coefs", coefs_hbm, coefs),
            ("static", static_hbm, static),
            ("scale", scale_hbm, scale),
            ("weight", weight_hbm, weight),
            ("innov", innov_hbm, innov),
        )
    ):
        loads[name] = pltpu.make_async_copy(source, target, in_sem.at[place])
    for name in ("control", "lat", "lon", "perts"):
        loads[name].start()
    barrier = pltpu.get_barrier_semaphore()
    for d in range(1, n):
        pl.semaphore_signal(
            barrier, inc=1, device_id={"tile": lax.rem(me + d, n)}, device_id_type=MESH
        )
    for name in ("coefs", "static", "scale", "weight", "innov"):
        loads[name].start()
    level_load = pltpu.make_async_copy(level_hbm, level_map, out_sem.at[2])
    level_load.start()

    loads["control"].wait()
    loads["lat"].wait()
    smoothed = jnp.dot(
        lat[...], control[...].astype(jnp.bfloat16), preferred_element_type=jnp.float32
    ).astype(jnp.bfloat16)
    loads["lon"].wait()
    member = lax.dot_general(
        smoothed, lon[...], (((1,), (1,)), ((), ())), preferred_element_type=jnp.float32
    )
    loads["perts"].wait()
    field[0:SIDE, :] = jnp.zeros((SIDE, cols), jnp.float32)
    field[SIDE + nlat : 2 * SIDE + nlat, :] = jnp.zeros((SIDE, cols), jnp.float32)
    field[SIDE : SIDE + nlat, :] = perts[...].astype(jnp.float32) * member

    pl.semaphore_wait(barrier, n - 1)

    def window(tile):
        return pl.ds(pl.multiple_of(tile * rows, 8), win)

    order = sorted(range(1, n), key=lambda d: abs(2 * d - n))
    member_copies = []

    def send_members(distances):
        for d in distances:
            peer = lax.rem(me + d, n)
            copy = pltpu.make_async_remote_copy(
                src_ref=field.at[window(peer)],
                dst_ref=received.at[me],
                send_sem=member_send_sem.at[d],
                recv_sem=member_recv_sem.at[d],
                device_id={"tile": peer},
                device_id_type=MESH,
            )
            copy.start()
            member_copies.append(copy)

    send_members(order[: n // 2])

    loads["coefs"].wait()
    loads["static"].wait()
    loads["scale"].wait()

    def early_rows(pair, half, level):
        for k in range(4):
            early_send[0, level, 2 * k : 2 * k + 2, :] = coefs[k, level, rows - 2 : rows, :]
            early_send[1, level, 2 * k : 2 * k + 2, :] = coefs[k, level, 0:2, :]
        value = scale[level] * static[level]
        at = half * SIDE
        early_send[0, levels + pair, at : at + SIDE, :] = value[rows - SIDE : rows]
        early_send[1, levels + pair, at : at + SIDE, :] = value[0:SIDE]

    each_level(early_rows)

    def exchange(send, recv, send_sem, recv_sem, action, chunk=0, width=None):
        def one(side, target):
            part = (side,) if width is None else (side, pl.ds(chunk * width, width))
            return pltpu.make_async_remote_copy(
                src_ref=send.at[part],
                dst_ref=recv.at[part],
                send_sem=send_sem.at[side, chunk],
                recv_sem=recv_sem.at[side, chunk],
                device_id={"tile": target},
                device_id_type=MESH,
            )

        @pl.when(me < n - 1)
        def _():
            action(0, 1, functools.partial(one, target=me + 1))

        @pl.when(me > 0)
        def _():
            action(1, 0, functools.partial(one, target=me - 1))

    def start(out, back, one):
        one(out).start()

    def wait_recv(out, back, one):
        one(back).wait_recv()

    def wait_send(out, back, one):
        one(out).wait_send()

    early = (early_send, early_recv, early_send_sem, early_recv_sem)
    late = (late_send, late_recv, late_send_sem, late_recv_sem)
    exchange(*early, start)
    send_members(order[n // 2 :])
    received[me] = field[window(me), :]

    lat_t[...] = lat[...].astype(jnp.float32).T.astype(jnp.bfloat16)
    lat_store = pltpu.make_async_copy(lat_t, lat_out, out_sem.at[1])
    lat_store.start()
    loads["weight"].wait()
    loads["innov"].wait()
    edge = jnp.zeros((SIDE, cols), jnp.float32)

    def widen(pair, half, level):
        for k in range(4):
            coef_win[k, level, main, :] = coefs[k, level]
        total_win[level, main, :] = scale[level] * static[level]
        for k in range(STEPS):
            for target, source in ((weight_win, weight), (innov_win, innov)):
                target[k, level, 0:SIDE, :] = edge
                target[k, level, main, :] = source[k, level]
                target[k, level, SIDE + rows : win, :] = edge

    each_level(widen)

    level_load.wait()

    def find(level, carry):
        low, high = jnp.int32(n - 1), jnp.int32(0)
        for block in range(n):
            here = level_map[block] == level
            low = jnp.minimum(low, jnp.where(here, block, n - 1))
            high = jnp.maximum(high, jnp.where(here, block, 0))
        blocks_of[0, level] = low
        blocks_of[1, level] = high
        return carry

    lax.fori_loop(0, levels, find, 0)

    exchange(*early, wait_recv)

    @pl.when(me == 0)
    def _():
        early_recv[0] = jnp.zeros(early_recv.shape[1:], jnp.float32)
        late_recv[0] = jnp.zeros(late_recv.shape[1:], jnp.float32)

    @pl.when(me == n - 1)
    def _():
        early_recv[1] = jnp.zeros(early_recv.shape[1:], jnp.float32)
        late_recv[1] = jnp.zeros(late_recv.shape[1:], jnp.float32)

    def unpack_early(pair, half, level):
        for k in range(4):
            coef_win[k, level, 0 : SIDE - 2, :] = jnp.full(
                (SIDE - 2, cols), 1.0 if k == 0 else 0.0, jnp.float32
            )
            coef_win[k, level, SIDE - 2 : SIDE, :] = early_recv[0, level, 2 * k : 2 * k + 2, :]
            coef_win[k, level, SIDE + rows : SIDE + rows + 2, :] = early_recv[
                1, level, 2 * k : 2 * k + 2, :
            ]
            coef_win[k, level, SIDE + rows + 2 : win, :] = jnp.full(
                (SIDE - 2, cols), 1.0 if k == 1 else 0.0, jnp.float32
            )
        at = half * SIDE
        total_win[level, 0:SIDE, :] = early_recv[0, levels + pair, at : at + SIDE, :]
        total_win[level, SIDE + rows : win, :] = early_recv[1, levels + pair, at : at + SIDE, :]
        keep_win[level] = 1.0 - (
            coef_win[0, level] + coef_win[1, level] + coef_win[2, level] + coef_win[3, level]
        )

    each_level(unpack_early)

    for copy in member_copies:
        copy.wait_recv()

    def forward(pair, half, level):
        state = total_win[level] + (received[blocks_of[0, level]] + received[blocks_of[1, level]])
        c = [coef_win[k, level] for k in range(4)]
        keep = keep_win[level]
        for k in range(STEPS):
            state = (
                keep * state
                + c[0] * pltpu.roll(state, win - 1, 0)
                + c[1] * pltpu.roll(state, 1, 0)
                + c[2] * pltpu.roll(state, cols - 1, 1)
                + c[3] * pltpu.roll(state, 1, 1)
            )
            value = weight_win[k, level] * (state - innov_win[k, level])
            weighted[k, level] = value
            at = k * (k + 1) // 2
            low, high = SIDE, SIDE + rows
            near = min(k + 1, 2)
            late_send[0, level, at : at + near, :] = value[high - near : high]
            late_send[1, level, at : at + near, :] = value[low : low + near]
            if k == 2:
                late_send[0, level, at + 2 : at + 3, :] = (c[0] * value)[high - 3 : high - 2]
                late_send[1, level, at + 2 : at + 3, :] = (c[1] * value)[low + 2 : low + 3]

    each_level(
        forward,
        after=lambda pair: exchange(*late, start, pair, 2),
    )

    def backward(pair, half, level):
        for k in range(STEPS):
            at = k * (k + 1) // 2
            low, high = SIDE, SIDE + rows
            near = min(k + 1, 2)
            weighted[k, level, low - near : low, :] = late_recv[0, level, at : at + near, :]
            weighted[k, level, high : high + near, :] = late_recv[1, level, at : at + near, :]
            if k == 2:
                weighted[k, level, low - 3 : low - 2, :] = late_recv[0, level, at + 2 : at + 3, :]
                weighted[k, level, high + 2 : high + 3, :] = late_recv[
                    1, level, at + 2 : at + 3, :
                ]
        adjoint = weighted[STEPS - 1, level]
        c = [coef_win[k, level] for k in range(4)]
        for k in range(STEPS - 2, -2, -1):
            adjoint = (
                keep_win[level] * adjoint
                + pltpu.roll(c[0] * adjoint, 1, 0)
                + pltpu.roll(c[1] * adjoint, win - 1, 0)
                + pltpu.roll(c[2] * adjoint, 1, 1)
                + pltpu.roll(c[3] * adjoint, cols - 1, 1)
            )
            if k >= 0:
                adjoint = adjoint + weighted[k, level]
        grad[level] = adjoint[SIDE : SIDE + rows]

    each_level(backward, before=lambda pair: exchange(*late, wait_recv, pair, 2))

    grad_copies = []
    for d in order:
        peer = lax.rem(me + d, n)
        grad_send[d] = grad[level_map[peer]]
        copy = pltpu.make_async_remote_copy(
            src_ref=grad_send.at[d],
            dst_ref=grad_field.at[me],
            send_sem=grad_send_sem.at[d],
            recv_sem=grad_recv_sem.at[d],
            device_id={"tile": peer},
            device_id_type=MESH,
        )
        copy.start()
        grad_copies.append(copy)
    grad_send[0] = grad[level_map[me]]
    own_store = pltpu.make_async_copy(grad_send.at[0], grad_field.at[me], out_sem.at[3])
    own_store.start()

    static_new[...] = static[...] - step_size * (static[...] + scale[...] * grad[...])
    static_store = pltpu.make_async_copy(static_new, static_out, out_sem.at[0])
    static_store.start()

    for copy in member_copies:
        copy.wait_send()
    exchange(*early, wait_send)

    def sent(pair):
        exchange(*late, wait_send, pair, 2)

    each_level(lambda *_: None, before=sent)
    for copy in grad_copies:
        copy.wait_recv()
    for copy in grad_copies:
        copy.wait_send()
    lat_store.wait()
    own_store.wait()
    static_store.wait()


def finish_kernel(
    grad_hbm,
    lat_hbm,
    lon_hbm,
    perts_hbm,
    control_hbm,
    static_hbm,
    ens_out,
    static_out,
    gradient,
    lat_t,
    lon,
    perts,
    control,
    ens_new,
    static_new,
    in_sem,
    out_sem,
):
    loads = []
    for place, (source, target) in enumerate(
        (
            (grad_hbm, gradient),
            (perts_hbm.at[0], perts),
            (lat_hbm, lat_t),
            (lon_hbm, lon),
            (control_hbm.at[0], control),
            (static_hbm, static_new),
        )
    ):
        loads.append(pltpu.make_async_copy(source, target, in_sem.at[place]))
        loads[-1].start()
    loads[0].wait()
    loads[1].wait()
    nlat, cols = control.shape
    grad_field = gradient[...].reshape(nlat, cols)
    weighted_grad = (perts[...].astype(jnp.float32) * grad_field).astype(jnp.bfloat16)
    for load in loads[2:]:
        load.wait()
    stores = [pltpu.make_async_copy(static_new, static_out, out_sem.at[2])]
    stores[0].start()
    for part in range(2):
        here = slice(part * nlat // 2, (part + 1) * nlat // 2)
        adjoint_lat = jnp.dot(
            lat_t[here, :], weighted_grad, preferred_element_type=jnp.float32
        ).astype(jnp.bfloat16)
        member_grad = jnp.dot(adjoint_lat, lon[...], preferred_element_type=jnp.float32)
        ens_new[here, :] = control[here, :] - step_size * (control[here, :] + member_grad)
        stores.append(
            pltpu.make_async_copy(ens_new.at[here], ens_out.at[0, here], out_sem.at[part])
        )
        stores[-1].start()
    for store in stores:
        store.wait()


def fused(n, *args):
    level_map, loc_lat, loc_lon, ens_perts, ens_control, static_control = args[:6]
    nlat, cols = ens_control.shape[1:]
    levels, rows, _ = static_control.shape
    win = rows + 2 * SIDE
    f32, bf16 = jnp.float32, jnp.bfloat16
    anywhere = pl.BlockSpec(memory_space=pl.ANY)
    dma = pltpu.SemaphoreType.DMA
    fields = (levels, rows, cols)
    windows = (levels, win, cols)
    grad_field, static_new, lat_t = pl.pallas_call(
        functools.partial(kernel, n),
        out_shape=(
            jax.ShapeDtypeStruct((n, rows, cols), f32),
            jax.ShapeDtypeStruct(static_control.shape, f32),
            jax.ShapeDtypeStruct(loc_lat.shape, bf16),
        ),
        in_specs=[pl.BlockSpec(memory_space=pltpu.HBM)] * 10,
        out_specs=(anywhere, anywhere, anywhere),
        scratch_shapes=[
            pltpu.SMEM(level_map.shape, jnp.int32),
            pltpu.SMEM((2, levels), jnp.int32),
            pltpu.VMEM(loc_lat.shape, bf16),
            pltpu.VMEM(loc_lon.shape, bf16),
            pltpu.VMEM((nlat, cols), bf16),
            pltpu.VMEM((nlat, cols), f32),
            pltpu.VMEM(fields, f32),
            pltpu.VMEM(fields, f32),
            pltpu.VMEM((4,) + fields, f32),
            pltpu.VMEM((STEPS,) + fields, f32),
            pltpu.VMEM((STEPS,) + fields, f32),
            pltpu.VMEM(loc_lat.shape, bf16),
            pltpu.VMEM((nlat + 2 * SIDE, cols), f32),
            pltpu.VMEM((n, win, cols), f32),
            pltpu.VMEM((4,) + windows, f32),
            pltpu.VMEM(windows, f32),
            pltpu.VMEM(windows, f32),
            pltpu.VMEM((STEPS,) + windows, f32),
            pltpu.VMEM((STEPS,) + windows, f32),
            pltpu.VMEM((STEPS,) + windows, f32),
            pltpu.VMEM((2, levels + levels // 2, 8, cols), f32),
            pltpu.VMEM((2, levels + levels // 2, 8, cols), f32),
            pltpu.VMEM((2, levels, 8, cols), f32),
            pltpu.VMEM((2, levels, 8, cols), f32),
            pltpu.VMEM(fields, f32),
            pltpu.VMEM((n, rows, cols), f32),
            pltpu.VMEM(fields, f32),
            dma((9,)),
            dma((4,)),
            dma((n,)),
            dma((n,)),
            dma((2, 1)),
            dma((2, 1)),
            dma((2, levels // 2)),
            dma((2, levels // 2)),
            dma((n,)),
            dma((n,)),
        ],
        compiler_params=pltpu.CompilerParams(
            collective_id=0, has_side_effects=True
        ),
    )(*args)
    return pl.pallas_call(
        finish_kernel,
        out_shape=(
            jax.ShapeDtypeStruct(ens_control.shape, f32),
            jax.ShapeDtypeStruct(static_control.shape, f32),
        ),
        in_specs=[anywhere] * 6,
        out_specs=(anywhere, anywhere),
        scratch_shapes=[
            pltpu.VMEM((n, rows, cols), f32),
            pltpu.VMEM(loc_lat.shape, bf16),
            pltpu.VMEM(loc_lon.shape, bf16),
            pltpu.VMEM((nlat, cols), bf16),
            pltpu.VMEM((nlat, cols), f32),
            pltpu.VMEM((nlat, cols), f32),
            pltpu.VMEM(fields, f32),
            dma((6,)),
            dma((3,)),
        ],
    )(grad_field, lat_t, loc_lon, ens_perts, ens_control, static_new)


def device_program(n, *args):
    ens_control, static_control = args[4:6]
    levels, rows, cols = static_control.shape
    fits = (
        ens_control.shape[0] == 1
        and n == 2 * levels
        and rows % 8 == 0
        and rows * n == ens_control.shape[1]
        and cols % 128 == 0
        and levels % 2 == 0
        and STEPS == 3
    )
    return fused(n, *args) if fits else local(*args)


def solution(mesh):
    in_specs = (
        P(),
        P(),
        P(),
        P(("groups", "tile"), None, None),
        P(("groups", "tile"), None, None),
        P("groups", "tile", None),
        P("groups", "tile", None),
        P(None, "groups", "tile", None),
        P(None, "groups", "tile", None),
        P(None, "groups", "tile", None),
    )
    out_specs = (P(("groups", "tile"), None, None), P("groups", "tile", None))
    body = functools.partial(device_program, mesh.shape["tile"])
    return jax.shard_map(body, mesh=mesh, in_specs=in_specs, out_specs=out_specs, check_vma=False)
```

```python
import functools

import jax
import jax.numpy as jnp
from jax import lax
from jax.experimental import pallas as pl
from jax.experimental.pallas import tpu as pltpu
from jax.sharding import PartitionSpec as P

STEPS = 3


step_size = 0.15


def extended(block, sides, width):
    for axis, dim in sides:
        count = lax.axis_size(axis)
        forward = [(i, i + 1) for i in range(count - 1)]
        backward = [(target, source) for source, target in forward]
        low = lax.ppermute(
            lax.slice_in_dim(block, block.shape[dim] - width, None, axis=dim), axis, forward
        )
        high = lax.ppermute(lax.slice_in_dim(block, 0, width, axis=dim), axis, backward)
        block = jnp.concatenate([low, block, high], axis=dim)
    return block


def forward_step(state, coeffs):
    padded = extended(state, (("tile", 1),), 1)
    north_rows = padded[:, 2:]
    south_rows = padded[:, :-2]
    east_cells = jnp.roll(state, -1, 2)
    west_cells = jnp.roll(state, 1, 2)
    return (
        state
        + coeffs[0] * (north_rows - state)
        + coeffs[1] * (south_rows - state)
        + coeffs[2] * (east_cells - state)
        + coeffs[3] * (west_cells - state)
    )


def adjoint_step(adjoint, coeffs):
    coef_sum = coeffs[0] + coeffs[1] + coeffs[2] + coeffs[3]
    fluxes = jnp.stack([coeffs[0] * adjoint, coeffs[1] * adjoint])
    padded = extended(fluxes, (("tile", 2),), 1)
    north_flux = padded[0][:, :-2]
    south_flux = padded[1][:, 2:]
    return (
        (1.0 - coef_sum) * adjoint
        + north_flux
        + south_flux
        + jnp.roll(coeffs[2] * adjoint, 1, 2)
        + jnp.roll(coeffs[3] * adjoint, -1, 2)
    )


def window_gradient(total_incr, coefs, obs_weight, innovation):
    state = total_incr
    weighted = []
    for section in range(STEPS):
        state = forward_step(state, coefs)
        weighted.append(obs_weight[section] * (state - innovation[section]))
    adjoint = weighted[STEPS - 1]
    for section in range(STEPS - 2, -1, -1):
        adjoint = adjoint_step(adjoint, coefs) + weighted[section]
    return adjoint_step(adjoint, coefs)


def local(
    level_map,
    loc_lat,
    loc_lon,
    ens_perts,
    ens_control,
    static_control,
    static_scale,
    coefs,
    obs_weight,
    innovation,
):
    tile_count = lax.axis_size("tile")
    my_level = level_map[lax.axis_index("tile")]
    levels = static_control.shape[0]
    level_ids = jnp.arange(levels, dtype=jnp.int32)
    level_onehot = (level_map[:, None] == level_ids[None, :]).astype(jnp.float32)
    control = ens_control
    lat_smoothed = jnp.einsum(
        "ij,bjk->bik", loc_lat, control.astype(jnp.bfloat16), preferred_element_type=jnp.float32
    ).astype(jnp.bfloat16)
    member_field = jnp.einsum(
        "bij,kj->bik", lat_smoothed, loc_lon, preferred_element_type=jnp.float32
    )
    partial_value = jnp.sum(ens_perts.astype(jnp.float32) * member_field, axis=0)
    pieces = partial_value.reshape(tile_count, -1, partial_value.shape[1])
    received = lax.all_to_all(pieces, "tile", split_axis=0, concat_axis=0, tiled=True)
    ens_incr = jnp.einsum("dl,dij->lij", level_onehot, received, precision=lax.Precision.HIGHEST)
    total_incr = static_scale * static_control + ens_incr
    gradient = window_gradient(total_incr, coefs, obs_weight, innovation)
    static_control = static_control - step_size * (static_control + static_scale * gradient)
    gathered = lax.all_gather(gradient, "tile", axis=1, tiled=True)
    grad_field = lax.dynamic_index_in_dim(gathered, my_level, 0, keepdims=False)
    weighted_grad = (ens_perts.astype(jnp.float32) * grad_field[None]).astype(jnp.bfloat16)
    adjoint_lat = jnp.einsum(
        "ji,bjk->bik", loc_lat, weighted_grad, preferred_element_type=jnp.float32
    ).astype(jnp.bfloat16)
    member_grad = jnp.einsum(
        "bij,jk->bik", adjoint_lat, loc_lon, preferred_element_type=jnp.float32
    )
    control = control - step_size * (control + member_grad)
    return (control, static_control)


MESH = pl.DeviceIdType.MESH
SIDE = 4


def kernel(
    n,
    level_hbm,
    lat_hbm,
    lon_hbm,
    perts_hbm,
    control_hbm,
    static_hbm,
    scale_hbm,
    coefs_hbm,
    weight_hbm,
    innov_hbm,
    grad_field,
    static_out,
    lat_out,
    level_map,
    blocks_of,
    lat,
    lon,
    perts,
    control,
    static,
    scale,
    coefs,
    weight,
    innov,
    lat_t,
    field,
    received,
    coef_win,
    keep_win,
    total_win,
    weight_win,
    innov_win,
    weighted,
    early_send,
    early_recv,
    late_send,
    late_recv,
    grad,
    grad_send,
    static_new,
    in_sem,
    out_sem,
    member_send_sem,
    member_recv_sem,
    early_send_sem,
    early_recv_sem,
    late_send_sem,
    late_recv_sem,
    grad_send_sem,
    grad_recv_sem,
):
    me = lax.axis_index("tile")
    levels, rows, cols = static.shape
    nlat = control.shape[0]
    win = rows + 2 * SIDE
    main = slice(SIDE, SIDE + rows)

    def each_level(body, before=None, after=None, width=2):
        def some(chunk, carry):
            if before is not None:
                before(chunk)
            for at in range(width):
                body(chunk * (width // 2) + at // 2, at % 2, width * chunk + at)
            if after is not None:
                after(chunk)
            return carry

        lax.fori_loop(0, levels // width, some, 0)

    loads = {}
    for place, (name, source, target) in enumerate(
        (
            ("control", control_hbm.at[0], control),
            ("lat", lat_hbm, lat),
            ("lon", lon_hbm, lon),
            ("perts", perts_hbm.at[0], perts),
            ("coefs", coefs_hbm, coefs),
            ("static", static_hbm, static),
            ("scale", scale_hbm, scale),
            ("weight", weight_hbm, weight),
            ("innov", innov_hbm, innov),
        )
    ):
        loads[name] = pltpu.make_async_copy(source, target, in_sem.at[place])
    for name in ("control", "lat", "lon", "perts"):
        loads[name].start()
    barrier = pltpu.get_barrier_semaphore()
    for d in range(1, n):
        pl.semaphore_signal(
            barrier, inc=1, device_id={"tile": lax.rem(me + d, n)}, device_id_type=MESH
        )
    for name in ("coefs", "static", "scale", "weight", "innov"):
        loads[name].start()
    level_load = pltpu.make_async_copy(level_hbm, level_map, out_sem.at[2])
    level_load.start()

    loads["control"].wait()
    loads["lat"].wait()
    smoothed = jnp.dot(
        lat[...], control[...].astype(jnp.bfloat16), preferred_element_type=jnp.float32
    ).astype(jnp.bfloat16)
    loads["lon"].wait()
    member = lax.dot_general(
        smoothed, lon[...], (((1,), (1,)), ((), ())), preferred_element_type=jnp.float32
    )
    loads["perts"].wait()
    field[0:SIDE, :] = jnp.zeros((SIDE, cols), jnp.float32)
    field[SIDE + nlat : 2 * SIDE + nlat, :] = jnp.zeros((SIDE, cols), jnp.float32)
    field[SIDE : SIDE + nlat, :] = perts[...].astype(jnp.float32) * member

    pl.semaphore_wait(barrier, n - 1)

    def window(tile):
        return pl.ds(pl.multiple_of(tile * rows, 8), win)

    order = sorted(range(1, n), key=lambda d: abs(2 * d - n))
    member_copies = []

    def send_members(distances):
        for d in distances:
            peer = lax.rem(me + d, n)
            copy = pltpu.make_async_remote_copy(
                src_ref=field.at[window(peer)],
                dst_ref=received.at[me],
                send_sem=member_send_sem.at[d],
                recv_sem=member_recv_sem.at[d],
                device_id={"tile": peer},
                device_id_type=MESH,
            )
            copy.start()
            member_copies.append(copy)

    send_members(order[: n // 2])

    loads["coefs"].wait()
    loads["static"].wait()
    loads["scale"].wait()

    def early_rows(pair, half, level):
        for k in range(4):
            early_send[0, level, 2 * k : 2 * k + 2, :] = coefs[k, level, rows - 2 : rows, :]
            early_send[1, level, 2 * k : 2 * k + 2, :] = coefs[k, level, 0:2, :]
        value = scale[level] * static[level]
        at = half * SIDE
        early_send[0, levels + pair, at : at + SIDE, :] = value[rows - SIDE : rows]
        early_send[1, levels + pair, at : at + SIDE, :] = value[0:SIDE]

    each_level(early_rows)

    def exchange(send, recv, send_sem, recv_sem, action, chunk=0, width=None):
        def one(side, target):
            part = (side,) if width is None else (side, pl.ds(chunk * width, width))
            return pltpu.make_async_remote_copy(
                src_ref=send.at[part],
                dst_ref=recv.at[part],
                send_sem=send_sem.at[side, chunk],
                recv_sem=recv_sem.at[side, chunk],
                device_id={"tile": target},
                device_id_type=MESH,
            )

        @pl.when(me < n - 1)
        def _():
            action(0, 1, functools.partial(one, target=me + 1))

        @pl.when(me > 0)
        def _():
            action(1, 0, functools.partial(one, target=me - 1))

    def start(out, back, one):
        one(out).start()

    def wait_recv(out, back, one):
        one(back).wait_recv()

    def wait_send(out, back, one):
        one(out).wait_send()

    early = (early_send, early_recv, early_send_sem, early_recv_sem)
    late = (late_send, late_recv, late_send_sem, late_recv_sem)
    exchange(*early, start)
    send_members(order[n // 2 :])
    received[me] = field[window(me), :]

    lat_t[...] = lat[...].astype(jnp.float32).T.astype(jnp.bfloat16)
    lat_store = pltpu.make_async_copy(lat_t, lat_out, out_sem.at[1])
    lat_store.start()
    loads["weight"].wait()
    loads["innov"].wait()
    edge = jnp.zeros((SIDE, cols), jnp.float32)

    def widen(pair, half, level):
        for k in range(4):
            coef_win[k, level, main, :] = coefs[k, level]
        total_win[level, main, :] = scale[level] * static[level]
        for k in range(STEPS):
            for target, source in ((weight_win, weight), (innov_win, innov)):
                target[k, level, 0:SIDE, :] = edge
                target[k, level, main, :] = source[k, level]
                target[k, level, SIDE + rows : win, :] = edge

    each_level(widen)

    level_load.wait()

    def find(level, carry):
        low, high = jnp.int32(n - 1), jnp.int32(0)
        for block in range(n):
            here = level_map[block] == level
            low = jnp.minimum(low, jnp.where(here, block, n - 1))
            high = jnp.maximum(high, jnp.where(here, block, 0))
        blocks_of[0, level] = low
        blocks_of[1, level] = high
        return carry

    lax.fori_loop(0, levels, find, 0)

    exchange(*early, wait_recv)

    @pl.when(me == 0)
    def _():
        early_recv[0] = jnp.zeros(early_recv.shape[1:], jnp.float32)
        late_recv[0] = jnp.zeros(late_recv.shape[1:], jnp.float32)

    @pl.when(me == n - 1)
    def _():
        early_recv[1] = jnp.zeros(early_recv.shape[1:], jnp.float32)
        late_recv[1] = jnp.zeros(late_recv.shape[1:], jnp.float32)

    def unpack_early(pair, half, level):
        for k in range(4):
            coef_win[k, level, 0 : SIDE - 2, :] = jnp.full(
                (SIDE - 2, cols), 1.0 if k == 0 else 0.0, jnp.float32
            )
            coef_win[k, level, SIDE - 2 : SIDE, :] = early_recv[0, level, 2 * k : 2 * k + 2, :]
            coef_win[k, level, SIDE + rows : SIDE + rows + 2, :] = early_recv[
                1, level, 2 * k : 2 * k + 2, :
            ]
            coef_win[k, level, SIDE + rows + 2 : win, :] = jnp.full(
                (SIDE - 2, cols), 1.0 if k == 1 else 0.0, jnp.float32
            )
        at = half * SIDE
        total_win[level, 0:SIDE, :] = early_recv[0, levels + pair, at : at + SIDE, :]
        total_win[level, SIDE + rows : win, :] = early_recv[1, levels + pair, at : at + SIDE, :]
        keep_win[level] = 1.0 - (
            coef_win[0, level] + coef_win[1, level] + coef_win[2, level] + coef_win[3, level]
        )

    each_level(unpack_early)

    for copy in member_copies:
        copy.wait_recv()

    def forward(pair, half, level):
        state = total_win[level] + (received[blocks_of[0, level]] + received[blocks_of[1, level]])
        c = [coef_win[k, level] for k in range(4)]
        keep = keep_win[level]
        for k in range(STEPS):
            state = (
                keep * state
                + c[0] * pltpu.roll(state, win - 1, 0)
                + c[1] * pltpu.roll(state, 1, 0)
                + c[2] * pltpu.roll(state, cols - 1, 1)
                + c[3] * pltpu.roll(state, 1, 1)
            )
            value = weight_win[k, level] * (state - innov_win[k, level])
            weighted[k, level] = value
            at = k * (k + 1) // 2
            low, high = SIDE, SIDE + rows
            near = min(k + 1, 2)
            late_send[0, level, at : at + near, :] = value[high - near : high]
            late_send[1, level, at : at + near, :] = value[low : low + near]
            if k == 2:
                late_send[0, level, at + 2 : at + 3, :] = (c[0] * value)[high - 3 : high - 2]
                late_send[1, level, at + 2 : at + 3, :] = (c[1] * value)[low + 2 : low + 3]

    each_level(
        forward,
        after=lambda chunk: exchange(*late, start, chunk, 4),
        width=4,
    )

    def backward(pair, half, level):
        for k in range(STEPS):
            at = k * (k + 1) // 2
            low, high = SIDE, SIDE + rows
            near = min(k + 1, 2)
            weighted[k, level, low - near : low, :] = late_recv[0, level, at : at + near, :]
            weighted[k, level, high : high + near, :] = late_recv[1, level, at : at + near, :]
            if k == 2:
                weighted[k, level, low - 3 : low - 2, :] = late_recv[0, level, at + 2 : at + 3, :]
                weighted[k, level, high + 2 : high + 3, :] = late_recv[
                    1, level, at + 2 : at + 3, :
                ]
        adjoint = weighted[STEPS - 1, level]
        c = [coef_win[k, level] for k in range(4)]
        for k in range(STEPS - 2, -2, -1):
            adjoint = (
                keep_win[level] * adjoint
                + pltpu.roll(c[0] * adjoint, 1, 0)
                + pltpu.roll(c[1] * adjoint, win - 1, 0)
                + pltpu.roll(c[2] * adjoint, 1, 1)
                + pltpu.roll(c[3] * adjoint, cols - 1, 1)
            )
            if k >= 0:
                adjoint = adjoint + weighted[k, level]
        grad[level] = adjoint[SIDE : SIDE + rows]

    each_level(backward, before=lambda chunk: exchange(*late, wait_recv, chunk, 4), width=4)

    grad_copies = []
    for d in order:
        peer = lax.rem(me + d, n)
        grad_send[d] = grad[level_map[peer]]
        copy = pltpu.make_async_remote_copy(
            src_ref=grad_send.at[d],
            dst_ref=grad_field.at[me],
            send_sem=grad_send_sem.at[d],
            recv_sem=grad_recv_sem.at[d],
            device_id={"tile": peer},
            device_id_type=MESH,
        )
        copy.start()
        grad_copies.append(copy)
    grad_send[0] = grad[level_map[me]]
    own_store = pltpu.make_async_copy(grad_send.at[0], grad_field.at[me], out_sem.at[3])
    own_store.start()

    static_new[...] = static[...] - step_size * (static[...] + scale[...] * grad[...])
    static_store = pltpu.make_async_copy(static_new, static_out, out_sem.at[0])
    static_store.start()

    for copy in member_copies:
        copy.wait_send()
    exchange(*early, wait_send)

    def sent(chunk):
        exchange(*late, wait_send, chunk, 4)

    each_level(lambda *_: None, before=sent, width=4)
    for copy in grad_copies:
        copy.wait_recv()
    for copy in grad_copies:
        copy.wait_send()
    lat_store.wait()
    own_store.wait()
    static_store.wait()


def finish_kernel(
    grad_hbm,
    lat_hbm,
    lon_hbm,
    perts_hbm,
    control_hbm,
    static_hbm,
    ens_out,
    static_out,
    gradient,
    lat_t,
    lon,
    perts,
    control,
    ens_new,
    static_new,
    in_sem,
    out_sem,
):
    loads = []
    for place, (source, target) in enumerate(
        (
            (grad_hbm, gradient),
            (perts_hbm.at[0], perts),
            (lat_hbm, lat_t),
            (lon_hbm, lon),
            (control_hbm.at[0], control),
            (static_hbm, static_new),
        )
    ):
        loads.append(pltpu.make_async_copy(source, target, in_sem.at[place]))
        loads[-1].start()
    loads[0].wait()
    loads[1].wait()
    nlat, cols = control.shape
    grad_field = gradient[...].reshape(nlat, cols)
    weighted_grad = (perts[...].astype(jnp.float32) * grad_field).astype(jnp.bfloat16)
    for load in loads[2:]:
        load.wait()
    stores = [pltpu.make_async_copy(static_new, static_out, out_sem.at[2])]
    stores[0].start()
    for part in range(2):
        here = slice(part * nlat // 2, (part + 1) * nlat // 2)
        adjoint_lat = jnp.dot(
            lat_t[here, :], weighted_grad, preferred_element_type=jnp.float32
        ).astype(jnp.bfloat16)
        member_grad = jnp.dot(adjoint_lat, lon[...], preferred_element_type=jnp.float32)
        ens_new[here, :] = control[here, :] - step_size * (control[here, :] + member_grad)
        stores.append(
            pltpu.make_async_copy(ens_new.at[here], ens_out.at[0, here], out_sem.at[part])
        )
        stores[-1].start()
    for store in stores:
        store.wait()


def fused(n, *args):
    level_map, loc_lat, loc_lon, ens_perts, ens_control, static_control = args[:6]
    nlat, cols = ens_control.shape[1:]
    levels, rows, _ = static_control.shape
    win = rows + 2 * SIDE
    f32, bf16 = jnp.float32, jnp.bfloat16
    anywhere = pl.BlockSpec(memory_space=pl.ANY)
    dma = pltpu.SemaphoreType.DMA
    fields = (levels, rows, cols)
    windows = (levels, win, cols)
    grad_field, static_new, lat_t = pl.pallas_call(
        functools.partial(kernel, n),
        out_shape=(
            jax.ShapeDtypeStruct((n, rows, cols), f32),
            jax.ShapeDtypeStruct(static_control.shape, f32),
            jax.ShapeDtypeStruct(loc_lat.shape, bf16),
        ),
        in_specs=[pl.BlockSpec(memory_space=pltpu.HBM)] * 10,
        out_specs=(anywhere, anywhere, anywhere),
        scratch_shapes=[
            pltpu.SMEM(level_map.shape, jnp.int32),
            pltpu.SMEM((2, levels), jnp.int32),
            pltpu.VMEM(loc_lat.shape, bf16),
            pltpu.VMEM(loc_lon.shape, bf16),
            pltpu.VMEM((nlat, cols), bf16),
            pltpu.VMEM((nlat, cols), f32),
            pltpu.VMEM(fields, f32),
            pltpu.VMEM(fields, f32),
            pltpu.VMEM((4,) + fields, f32),
            pltpu.VMEM((STEPS,) + fields, f32),
            pltpu.VMEM((STEPS,) + fields, f32),
            pltpu.VMEM(loc_lat.shape, bf16),
            pltpu.VMEM((nlat + 2 * SIDE, cols), f32),
            pltpu.VMEM((n, win, cols), f32),
            pltpu.VMEM((4,) + windows, f32),
            pltpu.VMEM(windows, f32),
            pltpu.VMEM(windows, f32),
            pltpu.VMEM((STEPS,) + windows, f32),
            pltpu.VMEM((STEPS,) + windows, f32),
            pltpu.VMEM((STEPS,) + windows, f32),
            pltpu.VMEM((2, levels + levels // 2, 8, cols), f32),
            pltpu.VMEM((2, levels + levels // 2, 8, cols), f32),
            pltpu.VMEM((2, levels, 8, cols), f32),
            pltpu.VMEM((2, levels, 8, cols), f32),
            pltpu.VMEM(fields, f32),
            pltpu.VMEM((n, rows, cols), f32),
            pltpu.VMEM(fields, f32),
            dma((9,)),
            dma((4,)),
            dma((n,)),
            dma((n,)),
            dma((2, 1)),
            dma((2, 1)),
            dma((2, levels // 4)),
            dma((2, levels // 4)),
            dma((n,)),
            dma((n,)),
        ],
        compiler_params=pltpu.CompilerParams(
            collective_id=0, has_side_effects=True
        ),
    )(*args)
    return pl.pallas_call(
        finish_kernel,
        out_shape=(
            jax.ShapeDtypeStruct(ens_control.shape, f32),
            jax.ShapeDtypeStruct(static_control.shape, f32),
        ),
        in_specs=[anywhere] * 6,
        out_specs=(anywhere, anywhere),
        scratch_shapes=[
            pltpu.VMEM((n, rows, cols), f32),
            pltpu.VMEM(loc_lat.shape, bf16),
            pltpu.VMEM(loc_lon.shape, bf16),
            pltpu.VMEM((nlat, cols), bf16),
            pltpu.VMEM((nlat, cols), f32),
            pltpu.VMEM((nlat, cols), f32),
            pltpu.VMEM(fields, f32),
            dma((6,)),
            dma((3,)),
        ],
    )(grad_field, lat_t, loc_lon, ens_perts, ens_control, static_new)


def device_program(n, *args):
    ens_control, static_control = args[4:6]
    levels, rows, cols = static_control.shape
    fits = (
        ens_control.shape[0] == 1
        and n == 2 * levels
        and rows % 8 == 0
        and rows * n == ens_control.shape[1]
        and cols % 128 == 0
        and levels % 4 == 0
        and STEPS == 3
    )
    return fused(n, *args) if fits else local(*args)


def solution(mesh):
    in_specs = (
        P(),
        P(),
        P(),
        P(("groups", "tile"), None, None),
        P(("groups", "tile"), None, None),
        P("groups", "tile", None),
        P("groups", "tile", None),
        P(None, "groups", "tile", None),
        P(None, "groups", "tile", None),
        P(None, "groups", "tile", None),
    )
    out_specs = (P(("groups", "tile"), None, None), P("groups", "tile", None))
    body = functools.partial(device_program, mesh.shape["tile"])
    return jax.shard_map(body, mesh=mesh, in_specs=in_specs, out_specs=out_specs, check_vma=False)
```
